32 devices in a mesh: rows: 8 (over y, x, core), gz: 4 (over z).
Axes of the slice: x: 2, y: 2, z: 4, core: 2. Of those that a mesh axis runs over, the one named last changes fastest.
Arguments:
- plane_colour_samples: int32 [8, 3, 256, 2048], P('gz', None, 'rows'), may hold values from 0 to 255
- clarity_gain: float32 [8], P('gz'), may hold values from 0.01 to 4
Outputs:
- joined: float32 [3, 256, 2048], P(None, 'rows')
The draws below stay inside these ranges and needn't reach their ends.
All inputs are finite; a program needn't handle non-finite values.
Results may differ from the reference program's by a relative error of at most 0.000067.
Values sent between devices are 32-bit elements; how exact they have to be, the bound alone decides.
A program may use at most 64 MiB of HBM per device.

```python
import jax
import jax.numpy as jnp
from jax import lax

COLOURS = 3
COLS = 2048
PLANES = 8
HEIGHT = 256


def draw_clarity_gain(key, part):
    key = jax.random.fold_in(key, 7)
    spread = jax.random.uniform(key, (PLANES,), jnp.float32)
    return jnp.exp(jnp.log(0.01) + spread * (jnp.log(0.1) - jnp.log(0.01)))


def touch_ends(result, stream_key, low, high):
    longest = result.shape.index(max(result.shape))
    spots = []
    for shift in (0, 1):
        where = [jax.random.randint(jax.random.fold_in(stream_key, axis), (), 0, length) for axis, length in enumerate(result.shape)]
        where[longest] = (where[longest] + shift) % result.shape[longest]
        spots.append(tuple(where))
    return result.at[spots[0]].set(low).at[spots[1]].set(high)


def setup_inputs(seed: int = 0) -> dict:
    streams_of = jax.random.split(jax.random.key(seed), 3)
    return {
        "plane_colour_samples": touch_ends(jax.random.randint(streams_of[0], (PLANES, COLOURS, HEIGHT, COLS), 0, 256), jax.random.fold_in(streams_of[0], 1), 0, 255).astype(jnp.int32),
        "clarity_gain": draw_clarity_gain(jax.random.fold_in(streams_of[2], 71), 0),
    }


def pad_rows(field, width):
    return jnp.pad(field, [(0, 0)] * (field.ndim - 2) + [(width, width), (0, 0)])


def blur_rows(padded_image, count):
    return (padded_image[..., 0:count, :] + 4.0 * padded_image[..., 1:count + 1, :] + 6.0 * padded_image[..., 2:count + 2, :]
            + 4.0 * padded_image[..., 3:count + 3, :] + padded_image[..., 4:count + 4, :]) / 16.0


def blur_cols(field):
    count = field.shape[-1]
    padded_image = jnp.pad(field, [(0, 0)] * (field.ndim - 1) + [(2, 2)])
    return (padded_image[..., 0:count] + 4.0 * padded_image[..., 1:count + 1] + 6.0 * padded_image[..., 2:count + 2]
            + 4.0 * padded_image[..., 3:count + 3] + padded_image[..., 4:count + 4]) / 16.0


def upsampled_rows(padded_image, count):
    even = (padded_image[..., 0:count, :] + 6.0 * padded_image[..., 1:count + 1, :] + padded_image[..., 2:count + 2, :]) / 8.0
    odd = (padded_image[..., 1:count + 1, :] + padded_image[..., 2:count + 2, :]) / 2.0
    shape = even.shape[:-2] + (2 * count, even.shape[-1])
    return jnp.stack([even, odd], axis=-2).reshape(shape)


def up_cols(field):
    count = field.shape[-1]
    padded_image = jnp.pad(field, [(0, 0)] * (field.ndim - 1) + [(1, 1)])
    even = (padded_image[..., 0:count] + 6.0 * padded_image[..., 1:count + 1] + padded_image[..., 2:count + 2]) / 8.0
    odd = (padded_image[..., 1:count + 1] + padded_image[..., 2:count + 2]) / 2.0
    shape = field.shape[:-1] + (2 * count,)
    return jnp.stack([even, odd], axis=-1).reshape(shape)


def reduce_level(padded_image, count):
    return blur_cols(blur_rows(padded_image, count))[..., ::2, ::2]


def expand_level(padded_image, count):
    return up_cols(upsampled_rows(padded_image, count))


def plane_energy(plane):
    image = plane.astype(jnp.float32) / 255.0
    grey = 0.299 * image[0] + 0.587 * image[1] + 0.114 * image[2]
    side = jnp.pad(grey, ((1, 1), (1, 1)))
    lap = 4.0 * grey - side[:-2, 1:-1] - side[2:, 1:-1] - side[1:-1, :-2] - side[1:-1, 2:]
    squared = lap * lap
    rows_pad = jnp.pad(squared, ((4, 4), (0, 0)))
    count = squared.shape[0]
    summed = rows_pad[0:count]
    for shift in range(1, 9):
        summed = summed + rows_pad[shift:shift + count]
    cols_pad = jnp.pad(summed, ((0, 0), (4, 4)))
    width = squared.shape[1]
    sharpness_measure_field = cols_pad[:, 0:width]
    for shift in range(1, 9):
        sharpness_measure_field = sharpness_measure_field + cols_pad[:, shift:shift + width]
    return sharpness_measure_field


def reference(plane_colour_samples, clarity_gain):
    height = plane_colour_samples.shape[2]
    sharpness_measure_field = lax.map(plane_energy, plane_colour_samples)
    clarity_ratings = clarity_gain[:, None, None] * sharpness_measure_field
    weights0 = jax.nn.softmax(clarity_ratings, axis=0)

    def accumulate(carry, item):
        plane, weight = item
        image = plane.astype(jnp.float32) / 255.0
        level1 = reduce_level(pad_rows(image, 2), height)
        level2 = reduce_level(pad_rows(level1, 2), height // 2)
        detail0 = image - expand_level(pad_rows(level1, 1), height // 2)
        detail1 = level1 - expand_level(pad_rows(level2, 1), height // 4)
        weight0 = weight[None]
        weight1 = reduce_level(pad_rows(weight0, 2), height)
        weight_level2 = reduce_level(pad_rows(weight1, 2), height // 2)
        return (carry[0] + weight0 * detail0, carry[1] + weight1 * detail1, carry[2] + weight_level2 * level2), None

    start = (jnp.zeros((COLOURS, height, COLS), jnp.float32),
             jnp.zeros((COLOURS, height // 2, COLS // 2), jnp.float32),
             jnp.zeros((COLOURS, height // 4, COLS // 4), jnp.float32))
    blends, unused = lax.scan(accumulate, start, (plane_colour_samples, weights0))
    mixed_finest_band, mixed_coarse_band, blend2 = blends
    central_rows = mixed_coarse_band + expand_level(pad_rows(blend2, 1), height // 4)
    return mixed_finest_band + expand_level(pad_rows(central_rows, 1), height // 2)
```

```python
import functools

import jax
import jax.numpy as jnp
import ml_dtypes
import numpy as np
from jax import lax
from jax.experimental import pallas as pl
from jax.experimental.pallas import tpu as pltpu
from jax.sharding import PartitionSpec as P

MESH = pl.DeviceIdType.MESH
F32 = jnp.float32
BF16 = jnp.bfloat16
TAPS = (1 / 16, 4 / 16, 6 / 16, 4 / 16, 1 / 16)


def down_rows(rows_in):
    m = np.zeros((rows_in // 2, rows_in), np.float32)
    for i in range(rows_in // 2):
        for t, tap in enumerate(TAPS):
            if 0 <= 2 * i + t - 2 < rows_in:
                m[i, 2 * i + t - 2] = tap
    return m


def up_rows(rows_in, rows_out, first):
    m = np.zeros((rows_out, rows_in), np.float32)
    for i in range(rows_out):
        k = first + i // 2
        pairs = ((k - 1, 1 / 8), (k, 6 / 8), (k + 1, 1 / 8)) if i % 2 == 0 else ((k, 1 / 2), (k + 1, 1 / 2))
        for r, tap in pairs:
            if 0 <= r < rows_in:
                m[i, r] = tap
    return m


def down_block():
    m = np.zeros((768, 256), np.float32)
    for o in range(256):
        for t, tap in enumerate(TAPS):
            m[128 + 2 * o + t - 2, o] = tap
    return m


def up_block():
    m = np.zeros((512, 512), np.float32)
    for k in range(256):
        m[127 + k, 2 * k] = m[129 + k, 2 * k] = 1 / 8
        m[128 + k, 2 * k] = 6 / 8
        m[128 + k, 2 * k + 1] = m[129 + k, 2 * k + 1] = 1 / 2
    return m


def blocks(count, matrix):
    return np.kron(np.eye(count, dtype=np.float32), matrix)


def dot(a, b):
    return lax.dot_general(a, b, (((1,), (0,)), ((), ())), preferred_element_type=F32)


def terms(v):
    high = v.astype(BF16)
    return high, (v - high.astype(F32)).astype(BF16)


def col_down(sources, matrix, width, put):
    for j in range(width // 512):
        first = 512 * j - 128
        low, high = max(0, first), min(width, first + 768)
        taps = matrix[low - first : high - first, :]
        put(256 * j, 256, sum(dot(s(low, high), taps) for s in sources))


def col_up(sources, matrix, width, put):
    for j in range(width // 256):
        first = 256 * j - 128
        low, high = max(0, first), min(width, first + 512)
        taps = matrix[low - first : high - first, :]
        put(512 * j, 512, sum(dot(s(low, high), taps) for s in sources))


def row_apply(matrix, read, width, put):
    for low in range(0, width, 512):
        high, rest = terms(read(low, low + 512))
        put(low, 512, dot(matrix, high) + dot(matrix, rest))


def kernel(
    n_rows, n_gz, planes, colours, strip, width,
    x_ref, gain_ref, dcol_ref, ucol_ref, d1x_ref, d1w_ref, d2x_ref, d2w_ref, u2x_ref, u2b_ref, u1_ref,
    out_ref,
    grey, sq, xb, cext, l1, l2, sth, stl, up2, detail, logit, lse, lse_in, lse_fin, w0, cw, w1, w2, c1, part, part_in,
    h_send, h_recv, e_send, e_recv, eo_send, eo_recv, j_send, j_recv, jo_send, jo_recv,
):
    pc = planes * colours
    half, quarter = strip // 2, strip // 4
    ext0, ext1, ext2 = strip + 32, half + 16, quarter + 8
    w_half, w_quarter = width // 2, width // 4
    r = lax.axis_index("rows")
    z = lax.axis_index("gz")
    has_up, has_down = r > 0, r < n_rows - 1
    upper, lower = jnp.maximum(r - 1, 0), jnp.minimum(r + 1, n_rows - 1)
    left = z < n_gz // 2
    inward = jnp.where(left, z + 1, z - 1)
    has_outer = jnp.logical_and(z > 0, z < n_gz - 1)
    outward = jnp.where(has_outer, jnp.where(left, z - 1, z + 1), z)
    is_mid = jnp.logical_or(z == n_gz // 2 - 1, z == n_gz // 2)
    slot = jnp.where(is_mid, 1, 0)
    not_mid = jnp.logical_not(is_mid)

    barrier = pltpu.get_barrier_semaphore()

    def greet(cond, device):
        @pl.when(cond)
        def _():
            pl.semaphore_signal(barrier, inc=1, device_id=device, device_id_type=MESH)

    greet(has_up, {"rows": upper})
    greet(has_down, {"rows": lower})
    greet(has_outer, {"gz": outward})
    pl.semaphore_signal(barrier, inc=1, device_id={"gz": inward}, device_id_type=MESH)

    for p in range(planes):
        samples = [x_ref[p, c].astype(F32) for c in range(colours)]
        for c in range(colours):
            xb[pl.ds((p * colours + c) * strip, strip), :] = samples[c].astype(BF16)
        mixed = 0.299 * samples[0] + 0.587 * samples[1] + 0.114 * samples[2]
        grey[p, pl.ds(8, strip), :width] = mixed * (1.0 / 255.0)
        grey[p, pl.ds(8, strip), width:] = jnp.zeros((strip, 128), F32)

    @pl.when(jnp.logical_not(has_up))
    def _():
        grey[:, 0:8, :] = jnp.zeros((planes, 8, width + 128), F32)
        cext[:, :, 0:16, :] = jnp.zeros((planes, colours, 16, w_half), F32)
        w0[:, 0:16, :] = jnp.zeros((planes, 16, width), F32)

    @pl.when(jnp.logical_not(has_down))
    def _():
        grey[:, strip + 8 :, :] = jnp.zeros((planes, 8, width + 128), F32)
        cext[:, :, strip + 16 :, :] = jnp.zeros((planes, colours, 16, w_half), F32)
        w0[:, strip + 16 :, :] = jnp.zeros((planes, 16, width), F32)

    pl.semaphore_wait(
        barrier, 1 + has_up.astype(jnp.int32) + has_down.astype(jnp.int32) + has_outer.astype(jnp.int32)
    )

    def halo(kind, ref, lead, depth):
        def view(first):
            return ref.at[(slice(None),) * lead + (pl.ds(first, depth), slice(None))]

        def copies():
            up = pltpu.make_async_remote_copy(
                src_ref=view(depth), dst_ref=view(strip + depth),
                send_sem=h_send.at[kind, 0], recv_sem=h_recv.at[kind, 0],
                device_id={"rows": upper}, device_id_type=MESH,
            )
            down = pltpu.make_async_remote_copy(
                src_ref=view(strip), dst_ref=view(0),
                send_sem=h_send.at[kind, 1], recv_sem=h_recv.at[kind, 1],
                device_id={"rows": lower}, device_id_type=MESH,
            )
            return up, down

        def start():
            up, down = copies()
            pl.when(has_up)(up.start)
            pl.when(has_down)(down.start)

        def arrived():
            up, down = copies()
            pl.when(has_down)(up.wait_recv)
            pl.when(has_up)(down.wait_recv)

        def sent():
            up, down = copies()
            pl.when(has_up)(up.wait_send)
            pl.when(has_down)(down.wait_send)

        return start, arrived, sent

    def chain(own, arrive, final, send, recv, out_send, out_recv):
        def inner(view, k, s):
            return pltpu.make_async_remote_copy(
                src_ref=own.at[view], dst_ref=arrive.at[(s,) + view],
                send_sem=send.at[k], recv_sem=recv.at[s, k],
                device_id={"gz": inward}, device_id_type=MESH,
            )

        def outer(view, k):
            return pltpu.make_async_remote_copy(
                src_ref=final.at[view], dst_ref=final.at[view],
                send_sem=out_send.at[k], recv_sem=out_recv.at[k],
                device_id={"gz": outward}, device_id_type=MESH,
            )

        return inner, outer

    grey_start, grey_arrived, grey_sent = halo(0, grey, 1, 8)
    image_start, image_arrived, image_sent = halo(1, cext, 2, 16)
    weight_start, weight_arrived, weight_sent = halo(2, w0, 1, 16)
    e_inner, e_outer = chain(lse, lse_in, lse_fin, e_send, e_recv, eo_send, eo_recv)
    j_inner, j_outer = chain(part, part_in, out_ref, j_send, j_recv, jo_send, jo_recv)

    grey_start()

    def put_c(low, count, v):
        cext[:, :, pl.ds(16, strip), low : low + count] = (v * (1.0 / 255.0)).reshape(planes, colours, strip, count)

    col_down([lambda a, b: xb[:, a:b]], dcol_ref, width, put_c)
    image_start()

    grey_arrived()
    line = lax.broadcasted_iota(jnp.int32, (strip + 8, width + 128), 0) + (r * strip - 4)
    column = lax.broadcasted_iota(jnp.int32, (strip + 8, width + 128), 1)
    inside = (line >= 0) & (line < strip * n_rows) & (column < width)
    padded = width + 128
    for p in range(planes):
        centre = grey[p, pl.ds(4, strip + 8), :]
        lap = 4.0 * centre - grey[p, pl.ds(3, strip + 8), :] - grey[p, pl.ds(5, strip + 8), :]
        lap = lap - pltpu.roll(centre, 1, 1) - pltpu.roll(centre, padded - 1, 1)
        lap = jnp.where(inside, lap, 0.0)
        sq[...] = lap * lap
        total = sq[pl.ds(0, strip), :]
        for k in range(1, 9):
            total = total + sq[pl.ds(k, strip), :]
        two = total + pltpu.roll(total, 1, 1)
        four = two + pltpu.roll(two, 2, 1)
        eight = four + pltpu.roll(four, 4, 1)
        nine = eight + pltpu.roll(total, 8, 1)
        energy = pltpu.roll(nine, padded - 4, 1)
        logit[p] = energy[:, :width] * gain_ref[p]

    top = logit[0]
    for p in range(1, planes):
        top = jnp.maximum(top, logit[p])
    den = jnp.exp(logit[0] - top)
    for p in range(1, planes):
        den = den + jnp.exp(logit[p] - top)
    lse[...] = top + jnp.log(den)

    e_chunks = [(pl.ds(8 * t, 8), slice(None)) for t in range(strip // 8)]

    def merge(a, b):
        return jnp.maximum(a, b) + jnp.log(1.0 + jnp.exp(-jnp.abs(a - b)))

    for k, view in enumerate(e_chunks):
        @pl.when(has_outer)
        def _():
            e_inner(view, k, 0).wait_recv()
            lse[view] = merge(lse[view], lse_in[(0,) + view])

        e_inner(view, k, slot).start()

    image_arrived()

    def edge_mask(rows_ext, margin, rows_own):
        row = lax.broadcasted_iota(jnp.int32, (rows_ext, 512), 0) + (r * rows_own - margin)
        return ((row >= 0) & (row < rows_own * n_rows)).astype(F32)[None]

    mask1 = edge_mask(ext1, 8, half)
    mask2 = edge_mask(ext2, 4, quarter)
    for p in range(planes):
        def put_l1(low, count, v):
            l1[p, :, :, low : low + count] = v.reshape(colours, ext1, count) * mask1

        row_apply(d1x_ref[...], lambda a, b: cext[p, :, :, a:b].reshape(colours * ext0, b - a), w_half, put_l1)

    def stage(rows, low, count, v):
        sth[0:rows, low : low + count], stl[0:rows, low : low + count] = terms(v)

    def staged(rows):
        return [lambda a, b: sth[0:rows, a:b], lambda a, b: stl[0:rows, a:b]]

    full = colours * strip
    for p in range(planes):
        row_apply(
            u1_ref[...], lambda a, b: l1[p, :, :, a:b].reshape(colours * ext1, b - a), w_half,
            functools.partial(stage, full),
        )

        def put_detail(low, count, v):
            samples = xb[pl.ds(p * full, full), low : low + count].astype(F32)
            detail[p, :, :, low : low + count] = (samples * (1.0 / 255.0) - v).reshape(colours, strip, count)

        col_up(staged(full), ucol_ref, w_half, put_detail)

    for k, view in enumerate(e_chunks):
        @pl.when(is_mid)
        def _():
            e_inner(view, k, 1).wait_recv()
            lse_fin[view] = merge(lse[view], lse_in[(1,) + view])

        @pl.when(not_mid)
        def _():
            e_outer(view, k).wait_recv()

        pl.when(has_outer)(e_outer(view, k).start)

    for p in range(planes):
        w0[p, pl.ds(16, strip), :] = jnp.exp(logit[p] - lse_fin[...])
    weight_start()

    rows1 = pc * ext1
    l1_terms = [
        lambda a, b: terms(l1[:, :, :, a:b].reshape(rows1, b - a))[0],
        lambda a, b: terms(l1[:, :, :, a:b].reshape(rows1, b - a))[1],
    ]

    def put_c2(low, count, v):
        up2[:, low : low + count] = v

    col_down(l1_terms, dcol_ref, w_half, put_c2)

    def put_l2(low, count, v):
        l2[:, :, :, low : low + count] = (v.reshape(pc, ext2, count) * mask2).reshape(planes, colours, ext2, count)

    row_apply(d2x_ref[...], lambda a, b: up2[:, a:b], w_quarter, put_l2)
    row_apply(
        u2x_ref[...], lambda a, b: l2[:, :, :, a:b].reshape(pc * ext2, b - a), w_quarter,
        functools.partial(stage, rows1),
    )

    def put_up2(low, count, v):
        up2[:, low : low + count] = v

    col_up(staged(rows1), ucol_ref, w_quarter, put_up2)

    weight_arrived()
    w_rows = planes * ext0
    w_terms = [
        lambda a, b: terms(w0[:, :, a:b].reshape(w_rows, b - a))[0],
        lambda a, b: terms(w0[:, :, a:b].reshape(w_rows, b - a))[1],
    ]

    def put_cw(low, count, v):
        cw[0:w_rows, low : low + count] = v

    col_down(w_terms, dcol_ref, width, put_cw)

    def put_w1(low, count, v):
        w1[:, :, low : low + count] = v.reshape(planes, ext1, count) * mask1

    row_apply(d1w_ref[...], lambda a, b: cw[0:w_rows, a:b], w_half, put_w1)
    w1_rows = planes * ext1
    w1_terms = [
        lambda a, b: terms(w1[:, :, a:b].reshape(w1_rows, b - a))[0],
        lambda a, b: terms(w1[:, :, a:b].reshape(w1_rows, b - a))[1],
    ]

    def put_cw2(low, count, v):
        cw[0:w1_rows, low : low + count] = v

    col_down(w1_terms, dcol_ref, w_half, put_cw2)

    def put_w2(low, count, v):
        w2[:, :, low : low + count] = v.reshape(planes, ext2, count) * mask2

    row_apply(d2w_ref[...], lambda a, b: cw[0:w1_rows, a:b], w_quarter, put_w2)

    def read_b2(a, b):
        acc = w2[0, :, a:b][None] * l2[0, :, :, a:b]
        for p in range(1, planes):
            acc = acc + w2[p, :, a:b][None] * l2[p, :, :, a:b]
        return acc.reshape(colours * ext2, b - a)

    rows_c1 = colours * ext1
    row_apply(u2b_ref[...], read_b2, w_quarter, functools.partial(stage, rows_c1))

    def put_c1(low, count, v):
        acc = v.reshape(colours, ext1, count)
        for p in range(planes):
            first = p * rows_c1
            coarse = up2[pl.ds(first, rows_c1), low : low + count].reshape(colours, ext1, count)
            acc = acc + w1[p, :, low : low + count][None] * (l1[p, :, :, low : low + count] - coarse)
        c1[:, :, low : low + count] = acc * mask1

    col_up(staged(rows_c1), ucol_ref, w_quarter, put_c1)

    row_apply(
        u1_ref[...], lambda a, b: c1[:, :, a:b].reshape(rows_c1, b - a), w_half, functools.partial(stage, full)
    )

    def put_part(low, count, v):
        acc = v.reshape(colours, strip, count)
        for p in range(planes):
            acc = acc + w0[p, pl.ds(16, strip), low : low + count][None] * detail[p, :, :, low : low + count]
        part[:, :, low : low + count] = acc

    col_up(staged(full), ucol_ref, w_half, put_part)

    j_chunks = [(c, pl.ds(8 * t, 8), slice(None)) for c in range(colours) for t in range(strip // 8)]

    def into(k):
        view = j_chunks[k]

        @pl.when(has_outer)
        def _():
            j_inner(view, k, 0).wait_recv()
            part[view] = part[view] + part_in[(0,) + view]

        j_inner(view, k, slot).start()

    def back(k):
        view = j_chunks[k]

        @pl.when(is_mid)
        def _():
            j_inner(view, k, 1).wait_recv()
            out_ref[view] = part[view] + part_in[(1,) + view]

        @pl.when(not_mid)
        def _():
            j_outer(view, k).wait_recv()

        pl.when(has_outer)(j_outer(view, k).start)

    lag = 2
    for k in range(len(j_chunks) + lag):
        if k < len(j_chunks):
            into(k)
        if k >= lag:
            back(k - lag)

    grey_sent()
    image_sent()
    weight_sent()
    for k, view in enumerate(e_chunks):
        e_inner(view, k, slot).wait_send()
        pl.when(has_outer)(e_outer(view, k).wait_send)
    for k, view in enumerate(j_chunks):
        j_inner(view, k, slot).wait_send()
        pl.when(has_outer)(j_outer(view, k).wait_send)


def on_device(n_rows, n_gz, samples, gain):
    planes, colours, strip, width = samples.shape
    pc = planes * colours
    half, quarter = strip // 2, strip // 4
    ext0, ext1, ext2 = strip + 32, half + 16, quarter + 8
    d1, d2 = down_rows(ext0), down_rows(ext1)
    u2, u1 = up_rows(ext2, ext1, 0), up_rows(ext1, strip, 8)
    constants = [
        down_block(), up_block(), blocks(colours, d1), blocks(planes, d1), blocks(pc, d2), blocks(planes, d2),
        blocks(pc, u2), blocks(colours, u2), blocks(colours, u1),
    ]
    constants = [jnp.asarray(c.astype(ml_dtypes.bfloat16)) for c in constants]
    n_e, n_j = strip // 8, colours * strip // 8
    dma = pltpu.SemaphoreType.DMA
    vmem = pl.BlockSpec(memory_space=pltpu.VMEM)
    return pl.pallas_call(
        functools.partial(kernel, n_rows, n_gz, planes, colours, strip, width),
        out_shape=jax.ShapeDtypeStruct((colours, strip, width), F32),
        in_specs=[vmem, pl.BlockSpec(memory_space=pltpu.SMEM)] + [vmem] * len(constants),
        out_specs=vmem,
        scratch_shapes=[
            pltpu.VMEM((planes, strip + 16, width + 128), F32),
            pltpu.VMEM((strip + 8, width + 128), F32),
            pltpu.VMEM((pc * strip, width), BF16),
            pltpu.VMEM((planes, colours, ext0, width // 2), F32),
            pltpu.VMEM((planes, colours, ext1, width // 2), F32),
            pltpu.VMEM((planes, colours, ext2, width // 4), F32),
            pltpu.VMEM((max(pc * ext1, colours * strip), width // 2), BF16),
            pltpu.VMEM((max(pc * ext1, colours * strip), width // 2), BF16),
            pltpu.VMEM((pc * ext1, width // 2), F32),
            pltpu.VMEM((planes, colours, strip, width), F32),
            pltpu.VMEM((planes, strip, width), F32),
            pltpu.VMEM((strip, width), F32),
            pltpu.VMEM((2, strip, width), F32),
            pltpu.VMEM((strip, width), F32),
            pltpu.VMEM((planes, ext0, width), F32),
            pltpu.VMEM((planes * ext0, width // 2), F32),
            pltpu.VMEM((planes, ext1, width // 2), F32),
            pltpu.VMEM((planes, ext2, width // 4), F32),
            pltpu.VMEM((colours, ext1, width // 2), F32),
            pltpu.VMEM((colours, strip, width), F32),
            pltpu.VMEM((2, colours, strip, width), F32),
            dma((3, 2)), dma((3, 2)),
            dma((n_e,)), dma((2, n_e)), dma((n_e,)), dma((n_e,)),
            dma((n_j,)), dma((2, n_j)), dma((n_j,)), dma((n_j,)),
        ],
        compiler_params=pltpu.CompilerParams(
            collective_id=0, has_side_effects=True, vmem_limit_bytes=48 * 1024 * 1024
        ),
    )(samples, gain, *constants)


def solution(mesh):
    return jax.shard_map(
        functools.partial(on_device, mesh.shape["rows"], mesh.shape["gz"]),
        mesh=mesh,
        in_specs=(P("gz", None, "rows", None), P("gz")),
        out_specs=P(None, "rows", None),
        check_vma=False,
    )
```

```python
import functools

import jax
import jax.numpy as jnp
import ml_dtypes
import numpy as np
from jax import lax
from jax.experimental import pallas as pl
from jax.experimental.pallas import tpu as pltpu
from jax.sharding import PartitionSpec as P

MESH = pl.DeviceIdType.MESH
F32 = jnp.float32
BF16 = jnp.bfloat16
TAPS = (1 / 16, 4 / 16, 6 / 16, 4 / 16, 1 / 16)


def down_rows(rows_in):
    m = np.zeros((rows_in // 2, rows_in), np.float32)
    for i in range(rows_in // 2):
        for t, tap in enumerate(TAPS):
            if 0 <= 2 * i + t - 2 < rows_in:
                m[i, 2 * i + t - 2] = tap
    return m


def up_rows(rows_in, rows_out, first):
    m = np.zeros((rows_out, rows_in), np.float32)
    for i in range(rows_out):
        k = first + i // 2
        pairs = ((k - 1, 1 / 8), (k, 6 / 8), (k + 1, 1 / 8)) if i % 2 == 0 else ((k, 1 / 2), (k + 1, 1 / 2))
        for r, tap in pairs:
            if 0 <= r < rows_in:
                m[i, r] = tap
    return m


def down_block():
    m = np.zeros((768, 256), np.float32)
    for o in range(256):
        for t, tap in enumerate(TAPS):
            m[128 + 2 * o + t - 2, o] = tap
    return m


def up_block():
    m = np.zeros((512, 512), np.float32)
    for k in range(256):
        m[127 + k, 2 * k] = m[129 + k, 2 * k] = 1 / 8
        m[128 + k, 2 * k] = 6 / 8
        m[128 + k, 2 * k + 1] = m[129 + k, 2 * k + 1] = 1 / 2
    return m


def blocks(count, matrix):
    return np.kron(np.eye(count, dtype=np.float32), matrix)


def dot(a, b):
    return lax.dot_general(a, b, (((1,), (0,)), ((), ())), preferred_element_type=F32)


def terms(v):
    high = v.astype(BF16)
    return high, (v - high.astype(F32)).astype(BF16)


def col_down(sources, matrix, width, put):
    for j in range(width // 512):
        first = 512 * j - 128
        low, high = max(0, first), min(width, first + 768)
        taps = matrix[low - first : high - first, :]
        put(256 * j, 256, sum(dot(s(low, high), taps) for s in sources))


def col_up(sources, matrix, width, put):
    for j in range(width // 256):
        first = 256 * j - 128
        low, high = max(0, first), min(width, first + 512)
        taps = matrix[low - first : high - first, :]
        put(512 * j, 512, sum(dot(s(low, high), taps) for s in sources))


def row_apply(matrix, read, width, put):
    for low in range(0, width, 512):
        high, rest = terms(read(low, low + 512))
        put(low, 512, dot(matrix, high) + dot(matrix, rest))


def kernel(
    n_rows, n_gz, planes, colours, strip, width,
    x_hbm, gain_ref, *refs,
):
    constants, out_ref, rest = refs[:9], refs[9], refs[10:]
    copied, rest = rest[:9], rest[9:]
    body(n_rows, n_gz, planes, colours, strip, width, x_hbm, gain_ref, constants, copied, out_ref, *rest)


def body(
    n_rows, n_gz, planes, colours, strip, width, x_hbm, gain_ref, constants, copied, out_ref,
    x_ref, x_sem, const_sem,
    grey, sq, xb, cext, l1, l2, sth, stl, up2, detail, logit, lse, lse_in, lse_fin, w0, cw, w1, w2, c1, part, part_in,
    h_send, h_recv, e_send, e_recv, eo_send, eo_recv, j_send, j_recv, jo_send, jo_recv,
):
    pc = planes * colours
    half, quarter = strip // 2, strip // 4
    ext0, ext1, ext2 = strip + 32, half + 16, quarter + 8
    w_half, w_quarter = width // 2, width // 4
    r = lax.axis_index("rows")
    z = lax.axis_index("gz")
    has_up, has_down = r > 0, r < n_rows - 1
    upper, lower = jnp.maximum(r - 1, 0), jnp.minimum(r + 1, n_rows - 1)
    left = z < n_gz // 2
    inward = jnp.where(left, z + 1, z - 1)
    has_outer = jnp.logical_and(z > 0, z < n_gz - 1)
    outward = jnp.where(has_outer, jnp.where(left, z - 1, z + 1), z)
    is_mid = jnp.logical_or(z == n_gz // 2 - 1, z == n_gz // 2)
    slot = jnp.where(is_mid, 1, 0)
    not_mid = jnp.logical_not(is_mid)

    dcol_ref, ucol_ref, d1x_ref, d1w_ref, d2x_ref, d2w_ref, u2x_ref, u2b_ref, u1_ref = copied
    loads = [pltpu.make_async_copy(x_hbm.at[p], x_ref.at[p], x_sem.at[p]) for p in range(planes)]
    fetches = [pltpu.make_async_copy(a, b, const_sem.at[k]) for k, (a, b) in enumerate(zip(constants, copied))]
    for copy in loads + fetches:
        copy.start()

    barrier = pltpu.get_barrier_semaphore()

    def greet(cond, device):
        @pl.when(cond)
        def _():
            pl.semaphore_signal(barrier, inc=1, device_id=device, device_id_type=MESH)

    greet(has_up, {"rows": upper})
    greet(has_down, {"rows": lower})
    greet(has_outer, {"gz": outward})
    pl.semaphore_signal(barrier, inc=1, device_id={"gz": inward}, device_id_type=MESH)

    for p in range(planes):
        loads[p].wait()
        samples = [x_ref[p, c].astype(F32) for c in range(colours)]
        for c in range(colours):
            xb[pl.ds((p * colours + c) * strip, strip), :] = samples[c].astype(BF16)
        mixed = 0.299 * samples[0] + 0.587 * samples[1] + 0.114 * samples[2]
        grey[p, pl.ds(8, strip), :width] = mixed * (1.0 / 255.0)
        grey[p, pl.ds(8, strip), width:] = jnp.zeros((strip, 128), F32)

    @pl.when(jnp.logical_not(has_up))
    def _():
        grey[:, 0:8, :] = jnp.zeros((planes, 8, width + 128), F32)
        cext[:, :, 0:16, :] = jnp.zeros((planes, colours, 16, w_half), F32)
        w0[:, 0:16, :] = jnp.zeros((planes, 16, width), F32)

    @pl.when(jnp.logical_not(has_down))
    def _():
        grey[:, strip + 8 :, :] = jnp.zeros((planes, 8, width + 128), F32)
        cext[:, :, strip + 16 :, :] = jnp.zeros((planes, colours, 16, w_half), F32)
        w0[:, strip + 16 :, :] = jnp.zeros((planes, 16, width), F32)

    pl.semaphore_wait(
        barrier, 1 + has_up.astype(jnp.int32) + has_down.astype(jnp.int32) + has_outer.astype(jnp.int32)
    )

    def halo(kind, ref, lead, depth):
        def view(first):
            return ref.at[(slice(None),) * lead + (pl.ds(first, depth), slice(None))]

        def copies():
            up = pltpu.make_async_remote_copy(
                src_ref=view(depth), dst_ref=view(strip + depth),
                send_sem=h_send.at[kind, 0], recv_sem=h_recv.at[kind, 0],
                device_id={"rows": upper}, device_id_type=MESH,
            )
            down = pltpu.make_async_remote_copy(
                src_ref=view(strip), dst_ref=view(0),
                send_sem=h_send.at[kind, 1], recv_sem=h_recv.at[kind, 1],
                device_id={"rows": lower}, device_id_type=MESH,
            )
            return up, down

        def start():
            up, down = copies()
            pl.when(has_up)(up.start)
            pl.when(has_down)(down.start)

        def arrived():
            up, down = copies()
            pl.when(has_down)(up.wait_recv)
            pl.when(has_up)(down.wait_recv)

        def sent():
            up, down = copies()
            pl.when(has_up)(up.wait_send)
            pl.when(has_down)(down.wait_send)

        return start, arrived, sent

    def chain(own, arrive, final, send, recv, out_send, out_recv):
        def inner(view, k, s):
            return pltpu.make_async_remote_copy(
                src_ref=own.at[view], dst_ref=arrive.at[(s,) + view],
                send_sem=send.at[k], recv_sem=recv.at[s, k],
                device_id={"gz": inward}, device_id_type=MESH,
            )

        def outer(view, k):
            return pltpu.make_async_remote_copy(
                src_ref=final.at[view], dst_ref=final.at[view],
                send_sem=out_send.at[k], recv_sem=out_recv.at[k],
                device_id={"gz": outward}, device_id_type=MESH,
            )

        return inner, outer

    grey_start, grey_arrived, grey_sent = halo(0, grey, 1, 8)
    image_start, image_arrived, image_sent = halo(1, cext, 2, 16)
    weight_start, weight_arrived, weight_sent = halo(2, w0, 1, 16)
    e_inner, e_outer = chain(lse, lse_in, lse_fin, e_send, e_recv, eo_send, eo_recv)
    j_inner, j_outer = chain(part, part_in, out_ref, j_send, j_recv, jo_send, jo_recv)

    grey_start()
    for copy in fetches:
        copy.wait()

    def put_c(low, count, v):
        cext[:, :, pl.ds(16, strip), low : low + count] = (v * (1.0 / 255.0)).reshape(planes, colours, strip, count)

    col_down([lambda a, b: xb[:, a:b]], dcol_ref, width, put_c)
    image_start()

    grey_arrived()
    line = lax.broadcasted_iota(jnp.int32, (strip + 8, width + 128), 0) + (r * strip - 4)
    column = lax.broadcasted_iota(jnp.int32, (strip + 8, width + 128), 1)
    inside = (line >= 0) & (line < strip * n_rows) & (column < width)
    padded = width + 128
    for p in range(planes):
        centre = grey[p, pl.ds(4, strip + 8), :]
        lap = 4.0 * centre - grey[p, pl.ds(3, strip + 8), :] - grey[p, pl.ds(5, strip + 8), :]
        lap = lap - pltpu.roll(centre, 1, 1) - pltpu.roll(centre, padded - 1, 1)
        lap = jnp.where(inside, lap, 0.0)
        sq[...] = lap * lap
        total = sq[pl.ds(0, strip), :]
        for k in range(1, 9):
            total = total + sq[pl.ds(k, strip), :]
        two = total + pltpu.roll(total, 1, 1)
        four = two + pltpu.roll(two, 2, 1)
        eight = four + pltpu.roll(four, 4, 1)
        nine = eight + pltpu.roll(total, 8, 1)
        energy = pltpu.roll(nine, padded - 4, 1)
        logit[p] = energy[:, :width] * gain_ref[p]

    top = logit[0]
    for p in range(1, planes):
        top = jnp.maximum(top, logit[p])
    den = jnp.exp(logit[0] - top)
    for p in range(1, planes):
        den = den + jnp.exp(logit[p] - top)
    lse[...] = top + jnp.log(den)

    e_chunks = [(pl.ds(8 * t, 8), slice(None)) for t in range(strip // 8)]

    def merge(a, b):
        return jnp.maximum(a, b) + jnp.log(1.0 + jnp.exp(-jnp.abs(a - b)))

    for k, view in enumerate(e_chunks):
        @pl.when(has_outer)
        def _():
            e_inner(view, k, 0).wait_recv()
            lse[view] = merge(lse[view], lse_in[(0,) + view])

        e_inner(view, k, slot).start()

    image_arrived()

    def edge_mask(rows_ext, margin, rows_own):
        row = lax.broadcasted_iota(jnp.int32, (rows_ext, 512), 0) + (r * rows_own - margin)
        return ((row >= 0) & (row < rows_own * n_rows)).astype(F32)[None]

    mask1 = edge_mask(ext1, 8, half)
    mask2 = edge_mask(ext2, 4, quarter)
    for p in range(planes):
        def put_l1(low, count, v):
            l1[p, :, :, low : low + count] = v.reshape(colours, ext1, count) * mask1

        row_apply(d1x_ref[...], lambda a, b: cext[p, :, :, a:b].reshape(colours * ext0, b - a), w_half, put_l1)

    def stage(rows, low, count, v):
        sth[0:rows, low : low + count], stl[0:rows, low : low + count] = terms(v)

    def staged(rows):
        return [lambda a, b: sth[0:rows, a:b], lambda a, b: stl[0:rows, a:b]]

    full = colours * strip
    for p in range(planes):
        row_apply(
            u1_ref[...], lambda a, b: l1[p, :, :, a:b].reshape(colours * ext1, b - a), w_half,
            functools.partial(stage, full),
        )

        def put_detail(low, count, v):
            samples = xb[pl.ds(p * full, full), low : low + count].astype(F32)
            detail[p, :, :, low : low + count] = (samples * (1.0 / 255.0) - v).reshape(colours, strip, count)

        col_up(staged(full), ucol_ref, w_half, put_detail)

    for k, view in enumerate(e_chunks):
        @pl.when(is_mid)
        def _():
            e_inner(view, k, 1).wait_recv()
            lse_fin[view] = merge(lse[view], lse_in[(1,) + view])

        @pl.when(not_mid)
        def _():
            e_outer(view, k).wait_recv()

        pl.when(has_outer)(e_outer(view, k).start)

    for p in range(planes):
        w0[p, pl.ds(16, strip), :] = jnp.exp(logit[p] - lse_fin[...])
    weight_start()

    rows1 = pc * ext1
    for low in range(0, w_half, 512):
        stage(rows1, low, 512, l1[:, :, :, low : low + 512].reshape(rows1, 512))

    def put_c2(low, count, v):
        up2[:, low : low + count] = v

    col_down(staged(rows1), dcol_ref, w_half, put_c2)

    def put_l2(low, count, v):
        l2[:, :, :, low : low + count] = (v.reshape(pc, ext2, count) * mask2).reshape(planes, colours, ext2, count)

    row_apply(d2x_ref[...], lambda a, b: up2[:, a:b], w_quarter, put_l2)
    row_apply(
        u2x_ref[...], lambda a, b: l2[:, :, :, a:b].reshape(pc * ext2, b - a), w_quarter,
        functools.partial(stage, rows1),
    )

    def put_up2(low, count, v):
        up2[:, low : low + count] = v

    col_up(staged(rows1), ucol_ref, w_quarter, put_up2)

    weight_arrived()
    w_rows = planes * ext0
    for low in range(0, width, 512):
        stage(w_rows, low, 512, w0[:, :, low : low + 512].reshape(w_rows, 512))

    def put_cw(low, count, v):
        cw[0:w_rows, low : low + count] = v

    col_down(staged(w_rows), dcol_ref, width, put_cw)

    def put_w1(low, count, v):
        w1[:, :, low : low + count] = v.reshape(planes, ext1, count) * mask1

    row_apply(d1w_ref[...], lambda a, b: cw[0:w_rows, a:b], w_half, put_w1)
    w1_rows = planes * ext1
    for low in range(0, w_half, 512):
        stage(w1_rows, low, 512, w1[:, :, low : low + 512].reshape(w1_rows, 512))

    def put_cw2(low, count, v):
        cw[0:w1_rows, low : low + count] = v

    col_down(staged(w1_rows), dcol_ref, w_half, put_cw2)

    def put_w2(low, count, v):
        w2[:, :, low : low + count] = v.reshape(planes, ext2, count) * mask2

    row_apply(d2w_ref[...], lambda a, b: cw[0:w1_rows, a:b], w_quarter, put_w2)

    def read_b2(a, b):
        acc = w2[0, :, a:b][None] * l2[0, :, :, a:b]
        for p in range(1, planes):
            acc = acc + w2[p, :, a:b][None] * l2[p, :, :, a:b]
        return acc.reshape(colours * ext2, b - a)

    rows_c1 = colours * ext1
    row_apply(u2b_ref[...], read_b2, w_quarter, functools.partial(stage, rows_c1))

    def put_c1(low, count, v):
        acc = v.reshape(colours, ext1, count)
        for p in range(planes):
            first = p * rows_c1
            coarse = up2[pl.ds(first, rows_c1), low : low + count].reshape(colours, ext1, count)
            acc = acc + w1[p, :, low : low + count][None] * (l1[p, :, :, low : low + count] - coarse)
        c1[:, :, low : low + count] = acc * mask1

    col_up(staged(rows_c1), ucol_ref, w_quarter, put_c1)

    row_apply(
        u1_ref[...], lambda a, b: c1[:, :, a:b].reshape(rows_c1, b - a), w_half, functools.partial(stage, full)
    )

    j_chunks = [(c, slice(None), slice(low, low + 512)) for low in range(0, width, 512) for c in range(colours)]

    def put_part(low, count, v):
        acc = v.reshape(colours, strip, count)
        for p in range(planes):
            acc = acc + w0[p, pl.ds(16, strip), low : low + count][None] * detail[p, :, :, low : low + count]
        part[:, :, low : low + count] = acc

        @pl.when(jnp.logical_not(has_outer))
        def _():
            for c in range(colours):
                k = low // count * colours + c
                j_inner(j_chunks[k], k, slot).start()

    col_up(staged(full), ucol_ref, w_half, put_part)

    def into(k):
        view = j_chunks[k]

        @pl.when(has_outer)
        def _():
            j_inner(view, k, 0).wait_recv()
            part[view] = part[view] + part_in[(0,) + view]
            j_inner(view, k, slot).start()

    def back(k):
        view = j_chunks[k]

        @pl.when(is_mid)
        def _():
            j_inner(view, k, 1).wait_recv()
            out_ref[view] = part[view] + part_in[(1,) + view]

        @pl.when(not_mid)
        def _():
            j_outer(view, k).wait_recv()

        pl.when(has_outer)(j_outer(view, k).start)

    lag = 4
    for k in range(len(j_chunks) + lag):
        if k < len(j_chunks):
            into(k)
        if k >= lag:
            back(k - lag)

    grey_sent()
    image_sent()
    weight_sent()
    for k, view in enumerate(e_chunks):
        e_inner(view, k, slot).wait_send()
        pl.when(has_outer)(e_outer(view, k).wait_send)
    for k, view in enumerate(j_chunks):
        j_inner(view, k, slot).wait_send()
        pl.when(has_outer)(j_outer(view, k).wait_send)


def on_device(n_rows, n_gz, samples, gain):
    planes, colours, strip, width = samples.shape
    pc = planes * colours
    half, quarter = strip // 2, strip // 4
    ext0, ext1, ext2 = strip + 32, half + 16, quarter + 8
    d1, d2 = down_rows(ext0), down_rows(ext1)
    u2, u1 = up_rows(ext2, ext1, 0), up_rows(ext1, strip, 8)
    constants = [
        down_block(), up_block(), blocks(colours, d1), blocks(planes, d1), blocks(pc, d2), blocks(planes, d2),
        blocks(pc, u2), blocks(colours, u2), blocks(colours, u1),
    ]
    constants = [jnp.asarray(c.astype(ml_dtypes.bfloat16)) for c in constants]
    n_e, n_j = strip // 8, colours * width // 512
    dma = pltpu.SemaphoreType.DMA
    vmem = pl.BlockSpec(memory_space=pltpu.VMEM)
    hbm = pl.BlockSpec(memory_space=pltpu.HBM)
    return pl.pallas_call(
        functools.partial(kernel, n_rows, n_gz, planes, colours, strip, width),
        out_shape=jax.ShapeDtypeStruct((colours, strip, width), F32),
        in_specs=[hbm, pl.BlockSpec(memory_space=pltpu.SMEM)] + [hbm] * len(constants),
        out_specs=vmem,
        scratch_shapes=[pltpu.VMEM(c.shape, c.dtype) for c in constants] + [
            pltpu.VMEM(samples.shape, samples.dtype),
            dma((planes,)), dma((len(constants),)),
            pltpu.VMEM((planes, strip + 16, width + 128), F32),
            pltpu.VMEM((strip + 8, width + 128), F32),
            pltpu.VMEM((pc * strip, width), BF16),
            pltpu.VMEM((planes, colours, ext0, width // 2), F32),
            pltpu.VMEM((planes, colours, ext1, width // 2), F32),
            pltpu.VMEM((planes, colours, ext2, width // 4), F32),
            pltpu.VMEM((max(pc * ext1, colours * strip, planes * ext0), width), BF16),
            pltpu.VMEM((max(pc * ext1, colours * strip, planes * ext0), width), BF16),
            pltpu.VMEM((pc * ext1, width // 2), F32),
            pltpu.VMEM((planes, colours, strip, width), F32),
            pltpu.VMEM((planes, strip, width), F32),
            pltpu.VMEM((strip, width), F32),
            pltpu.VMEM((2, strip, width), F32),
            pltpu.VMEM((strip, width), F32),
            pltpu.VMEM((planes, ext0, width), F32),
            pltpu.VMEM((planes * ext0, width // 2), F32),
            pltpu.VMEM((planes, ext1, width // 2), F32),
            pltpu.VMEM((planes, ext2, width // 4), F32),
            pltpu.VMEM((colours, ext1, width // 2), F32),
            pltpu.VMEM((colours, strip, width), F32),
            pltpu.VMEM((2, colours, strip, width), F32),
            dma((3, 2)), dma((3, 2)),
            dma((n_e,)), dma((2, n_e)), dma((n_e,)), dma((n_e,)),
            dma((n_j,)), dma((2, n_j)), dma((n_j,)), dma((n_j,)),
        ],
        compiler_params=pltpu.CompilerParams(
            collective_id=0, has_side_effects=True, vmem_limit_bytes=56 * 1024 * 1024
        ),
    )(samples, gain, *constants)


def solution(mesh):
    return jax.shard_map(
        functools.partial(on_device, mesh.shape["rows"], mesh.shape["gz"]),
        mesh=mesh,
        in_specs=(P("gz", None, "rows", None), P("gz")),
        out_specs=P(None, "rows", None),
        check_vma=False,
    )
```

```python
import functools

import jax
import jax.numpy as jnp
import ml_dtypes
import numpy as np
from jax import lax
from jax.experimental import pallas as pl
from jax.experimental.pallas import tpu as pltpu
from jax.sharding import PartitionSpec as P

MESH = pl.DeviceIdType.MESH
F32 = jnp.float32
BF16 = jnp.bfloat16
TAPS = (1 / 16, 4 / 16, 6 / 16, 4 / 16, 1 / 16)


def down_rows(rows_in):
    m = np.zeros((rows_in // 2, rows_in), np.float32)
    for i in range(rows_in // 2):
        for t, tap in enumerate(TAPS):
            if 0 <= 2 * i + t - 2 < rows_in:
                m[i, 2 * i + t - 2] = tap
    return m


def up_rows(rows_in, rows_out, first):
    m = np.zeros((rows_out, rows_in), np.float32)
    for i in range(rows_out):
        k = first + i // 2
        pairs = ((k - 1, 1 / 8), (k, 6 / 8), (k + 1, 1 / 8)) if i % 2 == 0 else ((k, 1 / 2), (k + 1, 1 / 2))
        for r, tap in pairs:
            if 0 <= r < rows_in:
                m[i, r] = tap
    return m


def down_block():
    m = np.zeros((768, 256), np.float32)
    for o in range(256):
        for t, tap in enumerate(TAPS):
            m[128 + 2 * o + t - 2, o] = tap
    return m


def up_block():
    m = np.zeros((512, 512), np.float32)
    for k in range(256):
        m[127 + k, 2 * k] = m[129 + k, 2 * k] = 1 / 8
        m[128 + k, 2 * k] = 6 / 8
        m[128 + k, 2 * k + 1] = m[129 + k, 2 * k + 1] = 1 / 2
    return m


def blocks(count, matrix):
    return np.kron(np.eye(count, dtype=np.float32), matrix)


def dot(a, b):
    return lax.dot_general(a, b, (((1,), (0,)), ((), ())), preferred_element_type=F32)


def terms(v):
    high = v.astype(BF16)
    return high, (v - high.astype(F32)).astype(BF16)


def col_down(sources, matrix, width, put):
    for j in range(width // 512):
        first = 512 * j - 128
        low, high = max(0, first), min(width, first + 768)
        taps = matrix[low - first : high - first, :]
        put(256 * j, 256, sum(dot(s(low, high), taps) for s in sources))


def col_up(sources, matrix, width, put):
    for j in range(width // 256):
        first = 256 * j - 128
        low, high = max(0, first), min(width, first + 512)
        taps = matrix[low - first : high - first, :]
        put(512 * j, 512, sum(dot(s(low, high), taps) for s in sources))


def row_apply(matrix, read, width, put):
    for low in range(0, width, 512):
        high, rest = terms(read(low, low + 512))
        put(low, 512, dot(matrix, high) + dot(matrix, rest))


def kernel(
    n_rows, n_gz, planes, colours, strip, width,
    x_hbm, gain_ref, *refs,
):
    constants, out_ref, rest = refs[:9], refs[9], refs[10:]
    copied, rest = rest[:9], rest[9:]
    body(n_rows, n_gz, planes, colours, strip, width, x_hbm, gain_ref, constants, copied, out_ref, *rest)


def body(
    n_rows, n_gz, planes, colours, strip, width, x_hbm, gain_ref, constants, copied, out_ref,
    x_ref, x_sem, const_sem,
    grey, sq, xb, cext, l1, l2, sth, stl, up2, detail, logit, lse, lse_in, lse_fin, w0, cw, cw2, w1, w2, c1, part, part_in,
    h_send, h_recv, e_send, e_recv, eo_send, eo_recv, j_send, j_recv, jo_send, jo_recv,
):
    pc = planes * colours
    half, quarter = strip // 2, strip // 4
    ext0, ext1, ext2 = strip + 32, half + 16, quarter + 8
    w_half, w_quarter = width // 2, width // 4
    r = lax.axis_index("rows")
    z = lax.axis_index("gz")
    has_up, has_down = r > 0, r < n_rows - 1
    upper, lower = jnp.maximum(r - 1, 0), jnp.minimum(r + 1, n_rows - 1)
    left = z < n_gz // 2
    inward = jnp.where(left, z + 1, z - 1)
    has_outer = jnp.logical_and(z > 0, z < n_gz - 1)
    outward = jnp.where(has_outer, jnp.where(left, z - 1, z + 1), z)
    is_mid = jnp.logical_or(z == n_gz // 2 - 1, z == n_gz // 2)
    slot = jnp.where(is_mid, 1, 0)
    not_mid = jnp.logical_not(is_mid)

    dcol_ref, ucol_ref, d1x_ref, d1w_ref, d2x_ref, d2w_ref, u2x_ref, u2b_ref, u1_ref = copied
    loads = [pltpu.make_async_copy(x_hbm.at[p], x_ref.at[p], x_sem.at[p]) for p in range(planes)]
    fetches = [pltpu.make_async_copy(a, b, const_sem.at[k]) for k, (a, b) in enumerate(zip(constants, copied))]
    for copy in loads + fetches:
        copy.start()

    barrier = pltpu.get_barrier_semaphore()

    def greet(cond, device):
        @pl.when(cond)
        def _():
            pl.semaphore_signal(barrier, inc=1, device_id=device, device_id_type=MESH)

    greet(has_up, {"rows": upper})
    greet(has_down, {"rows": lower})
    greet(has_outer, {"gz": outward})
    pl.semaphore_signal(barrier, inc=1, device_id={"gz": inward}, device_id_type=MESH)

    for p in range(planes):
        loads[p].wait()
        samples = [x_ref[p, c].astype(F32) for c in range(colours)]
        for c in range(colours):
            xb[pl.ds((p * colours + c) * strip, strip), :] = samples[c].astype(BF16)
        mixed = 0.299 * samples[0] + 0.587 * samples[1] + 0.114 * samples[2]
        grey[p, pl.ds(8, strip), :width] = mixed * (1.0 / 255.0)
        grey[p, pl.ds(8, strip), width:] = jnp.zeros((strip, 128), F32)

    @pl.when(jnp.logical_not(has_up))
    def _():
        grey[:, 0:8, :] = jnp.zeros((planes, 8, width + 128), F32)
        cext[:, :, 0:16, :] = jnp.zeros((planes, colours, 16, w_half), F32)
        cw[:, 0:16, :] = jnp.zeros((planes, 16, w_half), F32)

    @pl.when(jnp.logical_not(has_down))
    def _():
        grey[:, strip + 8 :, :] = jnp.zeros((planes, 8, width + 128), F32)
        cext[:, :, strip + 16 :, :] = jnp.zeros((planes, colours, 16, w_half), F32)
        cw[:, strip + 16 :, :] = jnp.zeros((planes, 16, w_half), F32)

    pl.semaphore_wait(
        barrier, 1 + has_up.astype(jnp.int32) + has_down.astype(jnp.int32) + has_outer.astype(jnp.int32)
    )

    def halo(kind, ref, lead, depth):
        def view(first):
            return ref.at[(slice(None),) * lead + (pl.ds(first, depth), slice(None))]

        def copies():
            up = pltpu.make_async_remote_copy(
                src_ref=view(depth), dst_ref=view(strip + depth),
                send_sem=h_send.at[kind, 0], recv_sem=h_recv.at[kind, 0],
                device_id={"rows": upper}, device_id_type=MESH,
            )
            down = pltpu.make_async_remote_copy(
                src_ref=view(strip), dst_ref=view(0),
                send_sem=h_send.at[kind, 1], recv_sem=h_recv.at[kind, 1],
                device_id={"rows": lower}, device_id_type=MESH,
            )
            return up, down

        def start():
            up, down = copies()
            pl.when(has_up)(up.start)
            pl.when(has_down)(down.start)

        def arrived():
            up, down = copies()
            pl.when(has_down)(up.wait_recv)
            pl.when(has_up)(down.wait_recv)

        def sent():
            up, down = copies()
            pl.when(has_up)(up.wait_send)
            pl.when(has_down)(down.wait_send)

        return start, arrived, sent

    def chain(own, arrive, final, send, recv, out_send, out_recv):
        def inner(view, k, s):
            return pltpu.make_async_remote_copy(
                src_ref=own.at[view], dst_ref=arrive.at[(s,) + view],
                send_sem=send.at[k], recv_sem=recv.at[s, k],
                device_id={"gz": inward}, device_id_type=MESH,
            )

        def outer(view, k):
            return pltpu.make_async_remote_copy(
                src_ref=final.at[view], dst_ref=final.at[view],
                send_sem=out_send.at[k], recv_sem=out_recv.at[k],
                device_id={"gz": outward}, device_id_type=MESH,
            )

        return inner, outer

    grey_start, grey_arrived, grey_sent = halo(0, grey, 1, 8)
    image_start, image_arrived, image_sent = halo(1, cext, 2, 16)
    weight_start, weight_arrived, weight_sent = halo(2, cw, 1, 16)
    e_inner, e_outer = chain(lse, lse_in, lse_fin, e_send, e_recv, eo_send, eo_recv)
    j_inner, j_outer = chain(part, part_in, out_ref, j_send, j_recv, jo_send, jo_recv)

    grey_start()

    padded = width + 128
    e_chunks = [(pl.ds(8 * t, 8), slice(None)) for t in range(strip // 8)]

    def square(p, i):
        line = lax.broadcasted_iota(jnp.int32, (8, padded), 0) + (r * strip - 4 + 8 * i)
        column = lax.broadcasted_iota(jnp.int32, (8, padded), 1)
        inside = (line >= 0) & (line < strip * n_rows) & (column < width)
        centre = grey[p, pl.ds(4 + 8 * i, 8), :]
        lap = 4.0 * centre - grey[p, pl.ds(3 + 8 * i, 8), :] - grey[p, pl.ds(5 + 8 * i, 8), :]
        lap = lap - pltpu.roll(centre, 1, 1) - pltpu.roll(centre, padded - 1, 1)
        lap = jnp.where(inside, lap, 0.0)
        sq[p, pl.ds(8 * i, 8), :] = lap * lap

    def merge(a, b):
        return jnp.maximum(a, b) + jnp.log(1.0 + jnp.exp(-jnp.abs(a - b)))

    def clarity(t):
        rows = pl.ds(8 * t, 8)
        top = None
        for p in range(planes):
            total = sq[p, rows, :]
            for k in range(1, 9):
                total = total + sq[p, pl.ds(8 * t + k, 8), :]
            two = total + pltpu.roll(total, 1, 1)
            four = two + pltpu.roll(two, 2, 1)
            eight = four + pltpu.roll(four, 4, 1)
            nine = eight + pltpu.roll(total, 8, 1)
            energy = pltpu.roll(nine, padded - 4, 1)
            scaled = energy[:, :width] * gain_ref[p]
            logit[p, rows, :] = scaled
            top = scaled if top is None else merge(top, scaled)
        lse[rows, :] = top

        @pl.when(jnp.logical_not(has_outer))
        def _():
            e_inner(e_chunks[t], t, slot).start()

    last = strip // 8
    for i in range(1, last):
        for p in range(planes):
            square(p, i)
    for t in range(1, last - 1):
        clarity(t)

    for copy in fetches:
        copy.wait()

    def put_c(low, count, v):
        cext[:, :, pl.ds(16, strip), low : low + count] = (v * (1.0 / 255.0)).reshape(planes, colours, strip, count)

    col_down([lambda a, b: xb[:, a:b]], dcol_ref, width, put_c)
    image_start()

    grey_arrived()
    for p in range(planes):
        square(p, 0)
        square(p, last)
    e_order = list(range(1, last - 1)) + sorted({0, last - 1})
    for t in e_order[last - 2 :]:
        clarity(t)

    @pl.when(has_outer)
    def _():
        for k in e_order:
            view = e_chunks[k]
            e_inner(view, k, 0).wait_recv()
            lse[view] = merge(lse[view], lse_in[(0,) + view])
            e_inner(view, k, slot).start()

    image_arrived()

    def edge_mask(rows_ext, margin, rows_own):
        row = lax.broadcasted_iota(jnp.int32, (rows_ext, 512), 0) + (r * rows_own - margin)
        return ((row >= 0) & (row < rows_own * n_rows)).astype(F32)[None]

    mask1 = edge_mask(ext1, 8, half)
    mask2 = edge_mask(ext2, 4, quarter)
    for p in range(planes):
        def put_l1(low, count, v):
            l1[p, :, :, low : low + count] = v.reshape(colours, ext1, count) * mask1

        row_apply(d1x_ref[...], lambda a, b: cext[p, :, :, a:b].reshape(colours * ext0, b - a), w_half, put_l1)

    def stage(rows, low, count, v):
        sth[0:rows, low : low + count], stl[0:rows, low : low + count] = terms(v)

    def staged(rows):
        return [lambda a, b: sth[0:rows, a:b], lambda a, b: stl[0:rows, a:b]]

    full = colours * strip
    for p in range(planes):
        row_apply(
            u1_ref[...], lambda a, b: l1[p, :, :, a:b].reshape(colours * ext1, b - a), w_half,
            functools.partial(stage, full),
        )

        def put_detail(low, count, v):
            samples = xb[pl.ds(p * full, full), low : low + count].astype(F32)
            detail[p, :, :, low : low + count] = (samples * (1.0 / 255.0) - v).reshape(colours, strip, count)

        col_up(staged(full), ucol_ref, w_half, put_detail)

    for k in e_order:
        view = e_chunks[k]

        @pl.when(is_mid)
        def _():
            e_inner(view, k, 1).wait_recv()
            lse_fin[view] = merge(lse[view], lse_in[(1,) + view])

        @pl.when(not_mid)
        def _():
            e_outer(view, k).wait_recv()

        pl.when(has_outer)(e_outer(view, k).start)
        for p in range(planes):
            w0[(p,) + view] = jnp.exp(logit[(p,) + view] - lse_fin[view])

    own_rows = planes * strip
    for low in range(0, width, 512):
        stage(own_rows, low, 512, w0[:, :, low : low + 512].reshape(own_rows, 512))

    def put_cw(low, count, v):
        cw[:, pl.ds(16, strip), low : low + count] = v.reshape(planes, strip, count)

    col_down(staged(own_rows), dcol_ref, width, put_cw)
    weight_start()

    for low in range(0, width, 512):
        for c in range(colours):
            acc = w0[0, :, low : low + 512] * detail[0, c, :, low : low + 512]
            for p in range(1, planes):
                acc = acc + w0[p, :, low : low + 512] * detail[p, c, :, low : low + 512]
            part[c, :, low : low + 512] = acc

    rows1 = pc * ext1
    for low in range(0, w_half, 512):
        stage(rows1, low, 512, l1[:, :, :, low : low + 512].reshape(rows1, 512))

    def put_c2(low, count, v):
        up2[:, low : low + count] = v

    col_down(staged(rows1), dcol_ref, w_half, put_c2)

    def put_l2(low, count, v):
        l2[:, :, :, low : low + count] = (v.reshape(pc, ext2, count) * mask2).reshape(planes, colours, ext2, count)

    row_apply(d2x_ref[...], lambda a, b: up2[:, a:b], w_quarter, put_l2)
    row_apply(
        u2x_ref[...], lambda a, b: l2[:, :, :, a:b].reshape(pc * ext2, b - a), w_quarter,
        functools.partial(stage, rows1),
    )

    def put_up2(low, count, v):
        up2[:, low : low + count] = v

    col_up(staged(rows1), ucol_ref, w_quarter, put_up2)

    weight_arrived()
    w_rows = planes * ext0

    def put_w1(low, count, v):
        w1[:, :, low : low + count] = v.reshape(planes, ext1, count) * mask1

    row_apply(d1w_ref[...], lambda a, b: cw[:, :, a:b].reshape(w_rows, b - a), w_half, put_w1)
    w1_rows = planes * ext1
    for low in range(0, w_half, 512):
        stage(w1_rows, low, 512, w1[:, :, low : low + 512].reshape(w1_rows, 512))

    def put_cw2(low, count, v):
        cw2[:, low : low + count] = v

    col_down(staged(w1_rows), dcol_ref, w_half, put_cw2)

    def put_w2(low, count, v):
        w2[:, :, low : low + count] = v.reshape(planes, ext2, count) * mask2

    row_apply(d2w_ref[...], lambda a, b: cw2[:, a:b], w_quarter, put_w2)

    def read_b2(a, b):
        acc = w2[0, :, a:b][None] * l2[0, :, :, a:b]
        for p in range(1, planes):
            acc = acc + w2[p, :, a:b][None] * l2[p, :, :, a:b]
        return acc.reshape(colours * ext2, b - a)

    rows_c1 = colours * ext1
    row_apply(u2b_ref[...], read_b2, w_quarter, functools.partial(stage, rows_c1))

    def put_c1(low, count, v):
        acc = v.reshape(colours, ext1, count)
        for p in range(planes):
            first = p * rows_c1
            coarse = up2[pl.ds(first, rows_c1), low : low + count].reshape(colours, ext1, count)
            acc = acc + w1[p, :, low : low + count][None] * (l1[p, :, :, low : low + count] - coarse)
        c1[:, :, low : low + count] = acc * mask1

    col_up(staged(rows_c1), ucol_ref, w_quarter, put_c1)

    row_apply(
        u1_ref[...], lambda a, b: c1[:, :, a:b].reshape(rows_c1, b - a), w_half, functools.partial(stage, full)
    )

    j_chunks = [(c, slice(None), slice(low, low + 512)) for low in range(0, width, 512) for c in range(colours)]

    def put_part(low, count, v):
        part[:, :, low : low + count] += v.reshape(colours, strip, count)

        @pl.when(jnp.logical_not(has_outer))
        def _():
            for c in range(colours):
                k = low // count * colours + c
                j_inner(j_chunks[k], k, slot).start()

    col_up(staged(full), ucol_ref, w_half, put_part)

    def into(k):
        view = j_chunks[k]

        @pl.when(has_outer)
        def _():
            j_inner(view, k, 0).wait_recv()
            part[view] = part[view] + part_in[(0,) + view]
            j_inner(view, k, slot).start()

    def back(k):
        view = j_chunks[k]

        @pl.when(is_mid)
        def _():
            j_inner(view, k, 1).wait_recv()
            out_ref[view] = part[view] + part_in[(1,) + view]

        @pl.when(not_mid)
        def _():
            j_outer(view, k).wait_recv()

        pl.when(has_outer)(j_outer(view, k).start)

    lag = 4
    for k in range(len(j_chunks) + lag):
        if k < len(j_chunks):
            into(k)
        if k >= lag:
            back(k - lag)

    grey_sent()
    image_sent()
    weight_sent()
    for k, view in enumerate(e_chunks):
        e_inner(view, k, slot).wait_send()
        pl.when(has_outer)(e_outer(view, k).wait_send)
    for k, view in enumerate(j_chunks):
        j_inner(view, k, slot).wait_send()
        pl.when(has_outer)(j_outer(view, k).wait_send)


def on_device(n_rows, n_gz, samples, gain):
    planes, colours, strip, width = samples.shape
    pc = planes * colours
    half, quarter = strip // 2, strip // 4
    ext0, ext1, ext2 = strip + 32, half + 16, quarter + 8
    d1, d2 = down_rows(ext0), down_rows(ext1)
    u2, u1 = up_rows(ext2, ext1, 0), up_rows(ext1, strip, 8)
    constants = [
        down_block(), up_block(), blocks(colours, d1), blocks(planes, d1), blocks(pc, d2), blocks(planes, d2),
        blocks(pc, u2), blocks(colours, u2), blocks(colours, u1),
    ]
    constants = [jnp.asarray(c.astype(ml_dtypes.bfloat16)) for c in constants]
    n_e, n_j = strip // 8, colours * width // 512
    dma = pltpu.SemaphoreType.DMA
    vmem = pl.BlockSpec(memory_space=pltpu.VMEM)
    hbm = pl.BlockSpec(memory_space=pltpu.HBM)
    return pl.pallas_call(
        functools.partial(kernel, n_rows, n_gz, planes, colours, strip, width),
        out_shape=jax.ShapeDtypeStruct((colours, strip, width), F32),
        in_specs=[hbm, pl.BlockSpec(memory_space=pltpu.SMEM)] + [hbm] * len(constants),
        out_specs=vmem,
        scratch_shapes=[pltpu.VMEM(c.shape, c.dtype) for c in constants] + [
            pltpu.VMEM(samples.shape, samples.dtype),
            dma((planes,)), dma((len(constants),)),
            pltpu.VMEM((planes, strip + 16, width + 128), F32),
            pltpu.VMEM((planes, strip + 8, width + 128), F32),
            pltpu.VMEM((pc * strip, width), BF16),
            pltpu.VMEM((planes, colours, ext0, width // 2), F32),
            pltpu.VMEM((planes, colours, ext1, width // 2), F32),
            pltpu.VMEM((planes, colours, ext2, width // 4), F32),
            pltpu.VMEM((max(pc * ext1, colours * strip, planes * ext0), width), BF16),
            pltpu.VMEM((max(pc * ext1, colours * strip, planes * ext0), width), BF16),
            pltpu.VMEM((pc * ext1, width // 2), F32),
            pltpu.VMEM((planes, colours, strip, width), F32),
            pltpu.VMEM((planes, strip, width), F32),
            pltpu.VMEM((strip, width), F32),
            pltpu.VMEM((2, strip, width), F32),
            pltpu.VMEM((strip, width), F32),
            pltpu.VMEM((planes, strip, width), F32),
            pltpu.VMEM((planes, ext0, width // 2), F32),
            pltpu.VMEM((planes * ext1, width // 4), F32),
            pltpu.VMEM((planes, ext1, width // 2), F32),
            pltpu.VMEM((planes, ext2, width // 4), F32),
            pltpu.VMEM((colours, ext1, width // 2), F32),
            pltpu.VMEM((colours, strip, width), F32),
            pltpu.VMEM((2, colours, strip, width), F32),
            dma((3, 2)), dma((3, 2)),
            dma((n_e,)), dma((2, n_e)), dma((n_e,)), dma((n_e,)),
            dma((n_j,)), dma((2, n_j)), dma((n_j,)), dma((n_j,)),
        ],
        compiler_params=pltpu.CompilerParams(
            collective_id=0, has_side_effects=True, vmem_limit_bytes=56 * 1024 * 1024
        ),
    )(samples, gain, *constants)


def solution(mesh):
    return jax.shard_map(
        functools.partial(on_device, mesh.shape["rows"], mesh.shape["gz"]),
        mesh=mesh,
        in_specs=(P("gz", None, "rows", None), P("gz")),
        out_specs=P(None, "rows", None),
        check_vma=False,
    )
```

```python
import functools

import jax
import jax.numpy as jnp
import ml_dtypes
import numpy as np
from jax import lax
from jax.experimental import pallas as pl
from jax.experimental.pallas import tpu as pltpu
from jax.sharding import PartitionSpec as P

MESH = pl.DeviceIdType.MESH
F32 = jnp.float32
BF16 = jnp.bfloat16
TAPS = (1 / 16, 4 / 16, 6 / 16, 4 / 16, 1 / 16)


def down_rows(rows_in, rows_out, first):
    m = np.zeros((rows_out, rows_in), np.float32)
    for i in range(rows_out):
        for t, tap in enumerate(TAPS):
            if 0 <= first + 2 * i + t - 2 < rows_in:
                m[i, first + 2 * i + t - 2] = tap
    return m


def up_rows(rows_in, rows_out, first):
    m = np.zeros((rows_out, rows_in), np.float32)
    for i in range(rows_out):
        k = first + i // 2
        pairs = ((k - 1, 1 / 8), (k, 6 / 8), (k + 1, 1 / 8)) if i % 2 == 0 else ((k, 1 / 2), (k + 1, 1 / 2))
        for r, tap in pairs:
            if 0 <= r < rows_in:
                m[i, r] = tap
    return m


def down_block():
    m = np.zeros((768, 256), np.float32)
    for o in range(256):
        for t, tap in enumerate(TAPS):
            m[128 + 2 * o + t - 2, o] = tap
    return m


def up_block():
    m = np.zeros((512, 512), np.float32)
    for k in range(256):
        m[127 + k, 2 * k] = m[129 + k, 2 * k] = 1 / 8
        m[128 + k, 2 * k] = 6 / 8
        m[128 + k, 2 * k + 1] = m[129 + k, 2 * k + 1] = 1 / 2
    return m


def blocks(count, matrix):
    return np.kron(np.eye(count, dtype=np.float32), matrix)


def dot(a, b):
    return lax.dot_general(a, b, (((1,), (0,)), ((), ())), preferred_element_type=F32)


def terms(v):
    high = v.astype(BF16)
    return high, (v - high.astype(F32)).astype(BF16)


def col_down(sources, matrix, width, put):
    for j in range(width // 512):
        first = 512 * j - 128
        low, high = max(0, first), min(width, first + 768)
        taps = matrix[low - first : high - first, :]
        put(256 * j, 256, sum(dot(s(low, high), taps) for s in sources))


def col_up(sources, matrix, width, put):
    for j in range(width // 256):
        first = 256 * j - 128
        low, high = max(0, first), min(width, first + 512)
        taps = matrix[low - first : high - first, :]
        put(512 * j, 512, sum(dot(s(low, high), taps) for s in sources))


def row_apply(matrix, read, width, put):
    for low in range(0, width, 512):
        high, rest = terms(read(low, low + 512))
        put(low, 512, dot(matrix, high) + dot(matrix, rest))


def kernel(
    n_rows, n_gz, planes, colours, strip, width,
    x_hbm, gain_ref, *refs,
):
    constants, out_ref, rest = refs[:9], refs[9], refs[10:]
    copied, rest = rest[:9], rest[9:]
    body(n_rows, n_gz, planes, colours, strip, width, x_hbm, gain_ref, constants, copied, out_ref, *rest)


def body(
    n_rows, n_gz, planes, colours, strip, width, x_hbm, gain_ref, constants, copied, out_ref,
    x_ref, x_sem, const_sem,
    grey, sq, xb, cext, l1, l2, sth, stl, up2, detail, logit, lse, lse_in, lse_fin, w0, cw, cw2, w1, w2, c1, part, part_in,
    h_send, h_recv, e_send, e_recv, eo_send, eo_recv, j_send, j_recv, jo_send, jo_recv,
):
    pc = planes * colours
    half, quarter = strip // 2, strip // 4
    ext0, extc, ext1, ext2 = strip + 32, strip + 16, half + 16, quarter + 16
    w_half, w_quarter = width // 2, width // 4
    r = lax.axis_index("rows")
    z = lax.axis_index("gz")
    has_up, has_down = r > 0, r < n_rows - 1
    upper, lower = jnp.maximum(r - 1, 0), jnp.minimum(r + 1, n_rows - 1)
    left = z < n_gz // 2
    inward = jnp.where(left, z + 1, z - 1)
    has_outer = jnp.logical_and(z > 0, z < n_gz - 1)
    outward = jnp.where(has_outer, jnp.where(left, z - 1, z + 1), z)
    is_mid = jnp.logical_or(z == n_gz // 2 - 1, z == n_gz // 2)
    slot = jnp.where(is_mid, 1, 0)
    not_mid = jnp.logical_not(is_mid)

    dcol_ref, ucol_ref, d1x_ref, d1w_ref, d2x_ref, d2w_ref, u2x_ref, u2b_ref, u1_ref = copied
    loads = [pltpu.make_async_copy(x_hbm.at[p], x_ref.at[p], x_sem.at[p]) for p in range(planes)]
    fetches = [pltpu.make_async_copy(a, b, const_sem.at[k]) for k, (a, b) in enumerate(zip(constants, copied))]
    for copy in loads + fetches:
        copy.start()

    barrier = pltpu.get_barrier_semaphore()

    def greet(cond, device):
        @pl.when(cond)
        def _():
            pl.semaphore_signal(barrier, inc=1, device_id=device, device_id_type=MESH)

    greet(has_up, {"rows": upper})
    greet(has_down, {"rows": lower})
    greet(has_outer, {"gz": outward})
    pl.semaphore_signal(barrier, inc=1, device_id={"gz": inward}, device_id_type=MESH)

    for p in range(planes):
        loads[p].wait()
        samples = [x_ref[p, c].astype(F32) for c in range(colours)]
        for c in range(colours):
            xb[pl.ds((p * colours + c) * strip, strip), :] = samples[c].astype(BF16)
        mixed = 0.299 * samples[0] + 0.587 * samples[1] + 0.114 * samples[2]
        grey[p, pl.ds(8, strip), :width] = mixed * (1.0 / 255.0)
        grey[p, pl.ds(8, strip), width:] = jnp.zeros((strip, 128), F32)

    @pl.when(jnp.logical_not(has_up))
    def _():
        grey[:, 0:8, :] = jnp.zeros((planes, 8, width + 128), F32)
        cext[:, :, 0:8, :] = jnp.zeros((planes, colours, 8, w_half), F32)
        l2[:, :, 0:8, :] = jnp.zeros((planes, colours, 8, w_quarter), F32)
        cw[:, 0:16, :] = jnp.zeros((planes, 16, w_half), F32)

    @pl.when(jnp.logical_not(has_down))
    def _():
        grey[:, strip + 8 :, :] = jnp.zeros((planes, 8, width + 128), F32)
        cext[:, :, strip + 8 :, :] = jnp.zeros((planes, colours, 8, w_half), F32)
        l2[:, :, quarter + 8 :, :] = jnp.zeros((planes, colours, 8, w_quarter), F32)
        cw[:, strip + 16 :, :] = jnp.zeros((planes, 16, w_half), F32)

    pl.semaphore_wait(
        barrier, 1 + has_up.astype(jnp.int32) + has_down.astype(jnp.int32) + has_outer.astype(jnp.int32)
    )

    def halo(kind, ref, lead, depth, own):
        def view(first):
            return ref.at[(slice(None),) * lead + (pl.ds(first, depth), slice(None))]

        def copies():
            up = pltpu.make_async_remote_copy(
                src_ref=view(depth), dst_ref=view(own + depth),
                send_sem=h_send.at[kind, 0], recv_sem=h_recv.at[kind, 0],
                device_id={"rows": upper}, device_id_type=MESH,
            )
            down = pltpu.make_async_remote_copy(
                src_ref=view(own), dst_ref=view(0),
                send_sem=h_send.at[kind, 1], recv_sem=h_recv.at[kind, 1],
                device_id={"rows": lower}, device_id_type=MESH,
            )
            return up, down

        def start():
            up, down = copies()
            pl.when(has_up)(up.start)
            pl.when(has_down)(down.start)

        def arrived():
            up, down = copies()
            pl.when(has_down)(up.wait_recv)
            pl.when(has_up)(down.wait_recv)

        def sent():
            up, down = copies()
            pl.when(has_up)(up.wait_send)
            pl.when(has_down)(down.wait_send)

        return start, arrived, sent

    def chain(own, arrive, final, send, recv, out_send, out_recv):
        def inner(view, k, s):
            return pltpu.make_async_remote_copy(
                src_ref=own.at[view], dst_ref=arrive.at[(s,) + view],
                send_sem=send.at[k], recv_sem=recv.at[s, k],
                device_id={"gz": inward}, device_id_type=MESH,
            )

        def outer(view, k):
            return pltpu.make_async_remote_copy(
                src_ref=final.at[view], dst_ref=final.at[view],
                send_sem=out_send.at[k], recv_sem=out_recv.at[k],
                device_id={"gz": outward}, device_id_type=MESH,
            )

        return inner, outer

    grey_start, grey_arrived, grey_sent = halo(0, grey, 1, 8, strip)
    image_start, image_arrived, image_sent = halo(1, cext, 2, 8, strip)
    weight_start, weight_arrived, weight_sent = halo(2, cw, 1, 16, strip)
    coarse_start, coarse_arrived, coarse_sent = halo(3, l2, 2, 8, quarter)
    e_inner, e_outer = chain(lse, lse_in, lse_fin, e_send, e_recv, eo_send, eo_recv)
    j_inner, j_outer = chain(part, part_in, out_ref, j_send, j_recv, jo_send, jo_recv)

    grey_start()
    for copy in fetches:
        copy.wait()

    def put_c(low, count, v):
        cext[:, :, pl.ds(8, strip), low : low + count] = (v * (1.0 / 255.0)).reshape(planes, colours, strip, count)

    col_down([lambda a, b: xb[:, a:b]], dcol_ref, width, put_c)
    image_start()

    padded = width + 128
    e_chunks = [(pl.ds(8 * t, 8), slice(None)) for t in range(strip // 8)]

    def square(p, i):
        line = lax.broadcasted_iota(jnp.int32, (8, padded), 0) + (r * strip - 4 + 8 * i)
        column = lax.broadcasted_iota(jnp.int32, (8, padded), 1)
        inside = (line >= 0) & (line < strip * n_rows) & (column < width)
        centre = grey[p, pl.ds(4 + 8 * i, 8), :]
        lap = 4.0 * centre - grey[p, pl.ds(3 + 8 * i, 8), :] - grey[p, pl.ds(5 + 8 * i, 8), :]
        lap = lap - pltpu.roll(centre, 1, 1) - pltpu.roll(centre, padded - 1, 1)
        lap = jnp.where(inside, lap, 0.0)
        sq[p, pl.ds(8 * i, 8), :] = lap * lap

    def merge(a, b):
        return jnp.maximum(a, b) + jnp.log(1.0 + jnp.exp(-jnp.abs(a - b)))

    def clarity(t):
        rows = pl.ds(8 * t, 8)
        top = None
        for p in range(planes):
            total = sq[p, rows, :]
            for k in range(1, 9):
                total = total + sq[p, pl.ds(8 * t + k, 8), :]
            two = total + pltpu.roll(total, 1, 1)
            four = two + pltpu.roll(two, 2, 1)
            eight = four + pltpu.roll(four, 4, 1)
            nine = eight + pltpu.roll(total, 8, 1)
            energy = pltpu.roll(nine, padded - 4, 1)
            scaled = energy[:, :width] * gain_ref[p]
            logit[p, rows, :] = scaled
            top = scaled if top is None else merge(top, scaled)
        lse[rows, :] = top

        @pl.when(jnp.logical_not(has_outer))
        def _():
            e_inner(e_chunks[t], t, slot).start()

    last = strip // 8
    for i in range(1, last):
        for p in range(planes):
            square(p, i)
    for t in range(1, last - 1):
        clarity(t)

    grey_arrived()
    for p in range(planes):
        square(p, 0)
        square(p, last)
    e_order = list(range(1, last - 1)) + sorted({0, last - 1})
    for t in e_order[last - 2 :]:
        clarity(t)

    @pl.when(has_outer)
    def _():
        for k in e_order:
            view = e_chunks[k]
            e_inner(view, k, 0).wait_recv()
            lse[view] = merge(lse[view], lse_in[(0,) + view])
            e_inner(view, k, slot).start()

    image_arrived()

    def edge_mask(rows_ext, margin, rows_own):
        row = lax.broadcasted_iota(jnp.int32, (rows_ext, 512), 0) + (r * rows_own - margin)
        return ((row >= 0) & (row < rows_own * n_rows)).astype(F32)[None]

    mask1 = edge_mask(ext1, 8, half)
    mask2 = edge_mask(ext2, 8, quarter)
    for p in range(planes):
        def put_l1(low, count, v):
            l1[p, :, :, low : low + count] = v.reshape(colours, ext1, count) * mask1

        row_apply(d1x_ref[...], lambda a, b: cext[p, :, :, a:b].reshape(colours * extc, b - a), w_half, put_l1)

    def stage(rows, low, count, v):
        sth[0:rows, low : low + count], stl[0:rows, low : low + count] = terms(v)

    def staged(rows):
        return [lambda a, b: sth[0:rows, a:b], lambda a, b: stl[0:rows, a:b]]

    full = colours * strip
    for p in range(planes):
        row_apply(
            u1_ref[...], lambda a, b: l1[p, :, :, a:b].reshape(colours * ext1, b - a), w_half,
            functools.partial(stage, full),
        )

        def put_detail(low, count, v):
            samples = xb[pl.ds(p * full, full), low : low + count].astype(F32)
            detail[p, :, :, low : low + count] = (samples * (1.0 / 255.0) - v).reshape(colours, strip, count)

        col_up(staged(full), ucol_ref, w_half, put_detail)

    for k in e_order:
        view = e_chunks[k]

        @pl.when(is_mid)
        def _():
            e_inner(view, k, 1).wait_recv()
            lse_fin[view] = merge(lse[view], lse_in[(1,) + view])

        @pl.when(not_mid)
        def _():
            e_outer(view, k).wait_recv()

        pl.when(has_outer)(e_outer(view, k).start)
        for p in range(planes):
            w0[(p,) + view] = jnp.exp(logit[(p,) + view] - lse_fin[view])

    own_rows = planes * strip
    for low in range(0, width, 512):
        stage(own_rows, low, 512, w0[:, :, low : low + 512].reshape(own_rows, 512))

    def put_cw(low, count, v):
        cw[:, pl.ds(16, strip), low : low + count] = v.reshape(planes, strip, count)

    col_down(staged(own_rows), dcol_ref, width, put_cw)
    weight_start()

    def weighted_detail():
        for low in range(0, width, 512):
            for c in range(colours):
                acc = w0[0, :, low : low + 512] * detail[0, c, :, low : low + 512]
                for p in range(1, planes):
                    acc = acc + w0[p, :, low : low + 512] * detail[p, c, :, low : low + 512]
                part[c, :, low : low + 512] = acc

    rows1 = pc * ext1
    for low in range(0, w_half, 512):
        stage(rows1, low, 512, l1[:, :, :, low : low + 512].reshape(rows1, 512))

    def put_c2(low, count, v):
        up2[:, low : low + count] = v

    col_down(staged(rows1), dcol_ref, w_half, put_c2)

    def put_l2(low, count, v):
        l2[:, :, pl.ds(8, quarter), low : low + count] = v.reshape(planes, colours, quarter, count)

    row_apply(d2x_ref[...], lambda a, b: up2[:, a:b], w_quarter, put_l2)
    coarse_start()
    weighted_detail()
    coarse_arrived()
    row_apply(
        u2x_ref[...], lambda a, b: l2[:, :, :, a:b].reshape(pc * ext2, b - a), w_quarter,
        functools.partial(stage, rows1),
    )

    def put_up2(low, count, v):
        up2[:, low : low + count] = v

    col_up(staged(rows1), ucol_ref, w_quarter, put_up2)

    weight_arrived()
    w_rows = planes * ext0

    def put_w1(low, count, v):
        w1[:, :, low : low + count] = v.reshape(planes, ext1, count) * mask1

    row_apply(d1w_ref[...], lambda a, b: cw[:, :, a:b].reshape(w_rows, b - a), w_half, put_w1)
    w1_rows = planes * ext1
    for low in range(0, w_half, 512):
        stage(w1_rows, low, 512, w1[:, :, low : low + 512].reshape(w1_rows, 512))

    def put_cw2(low, count, v):
        cw2[:, low : low + count] = v

    col_down(staged(w1_rows), dcol_ref, w_half, put_cw2)

    def put_w2(low, count, v):
        w2[:, :, low : low + count] = v.reshape(planes, ext2, count) * mask2

    row_apply(d2w_ref[...], lambda a, b: cw2[:, a:b], w_quarter, put_w2)

    def read_b2(a, b):
        acc = w2[0, :, a:b][None] * l2[0, :, :, a:b]
        for p in range(1, planes):
            acc = acc + w2[p, :, a:b][None] * l2[p, :, :, a:b]
        return acc.reshape(colours * ext2, b - a)

    rows_c1 = colours * ext1
    row_apply(u2b_ref[...], read_b2, w_quarter, functools.partial(stage, rows_c1))

    def put_c1(low, count, v):
        acc = v.reshape(colours, ext1, count)
        for p in range(planes):
            first = p * rows_c1
            coarse = up2[pl.ds(first, rows_c1), low : low + count].reshape(colours, ext1, count)
            acc = acc + w1[p, :, low : low + count][None] * (l1[p, :, :, low : low + count] - coarse)
        c1[:, :, low : low + count] = acc * mask1

    col_up(staged(rows_c1), ucol_ref, w_quarter, put_c1)

    row_apply(
        u1_ref[...], lambda a, b: c1[:, :, a:b].reshape(rows_c1, b - a), w_half, functools.partial(stage, full)
    )

    j_chunks = [(c, slice(None), slice(low, low + 512)) for low in range(0, width, 512) for c in range(colours)]

    def into(k):
        view = j_chunks[k]

        @pl.when(has_outer)
        def _():
            j_inner(view, k, 0).wait_recv()
            part[view] = part[view] + part_in[(0,) + view]
            j_inner(view, k, slot).start()

    def put_part(low, count, v):
        part[:, :, low : low + count] += v.reshape(colours, strip, count)

        @pl.when(jnp.logical_not(has_outer))
        def _():
            for c in range(colours):
                k = low // count * colours + c
                j_inner(j_chunks[k], k, slot).start()

        for k in range(max(0, low // count - 1) * colours, low // count * colours):
            into(k)

    col_up(staged(full), ucol_ref, w_half, put_part)

    def back(k):
        view = j_chunks[k]

        @pl.when(is_mid)
        def _():
            j_inner(view, k, 1).wait_recv()
            out_ref[view] = part[view] + part_in[(1,) + view]

        @pl.when(not_mid)
        def _():
            j_outer(view, k).wait_recv()

        pl.when(has_outer)(j_outer(view, k).start)

    for k in range(len(j_chunks)):
        if k < colours:
            into(len(j_chunks) - colours + k)
        back(k)

    grey_sent()
    image_sent()
    coarse_sent()
    weight_sent()
    for k, view in enumerate(e_chunks):
        e_inner(view, k, slot).wait_send()
        pl.when(has_outer)(e_outer(view, k).wait_send)
    for k, view in enumerate(j_chunks):
        j_inner(view, k, slot).wait_send()
        pl.when(has_outer)(j_outer(view, k).wait_send)


def on_device(n_rows, n_gz, samples, gain):
    planes, colours, strip, width = samples.shape
    pc = planes * colours
    half, quarter = strip // 2, strip // 4
    ext0, extc, ext1, ext2 = strip + 32, strip + 16, half + 16, quarter + 16
    d1x, d1w = down_rows(extc, ext1, -8), down_rows(ext0, ext1, 0)
    d2x, d2w = down_rows(ext1, quarter, 8), down_rows(ext1, ext2, -8)
    u2, u1 = up_rows(ext2, ext1, 4), up_rows(ext1, strip, 8)
    constants = [
        down_block(), up_block(), blocks(colours, d1x), blocks(planes, d1w), blocks(pc, d2x), blocks(planes, d2w),
        blocks(pc, u2), blocks(colours, u2), blocks(colours, u1),
    ]
    constants = [jnp.asarray(c.astype(ml_dtypes.bfloat16)) for c in constants]
    n_e, n_j = strip // 8, colours * width // 512
    dma = pltpu.SemaphoreType.DMA
    vmem = pl.BlockSpec(memory_space=pltpu.VMEM)
    hbm = pl.BlockSpec(memory_space=pltpu.HBM)
    return pl.pallas_call(
        functools.partial(kernel, n_rows, n_gz, planes, colours, strip, width),
        out_shape=jax.ShapeDtypeStruct((colours, strip, width), F32),
        in_specs=[hbm, pl.BlockSpec(memory_space=pltpu.SMEM)] + [hbm] * len(constants),
        out_specs=vmem,
        scratch_shapes=[pltpu.VMEM(c.shape, c.dtype) for c in constants] + [
            pltpu.VMEM(samples.shape, samples.dtype),
            dma((planes,)), dma((len(constants),)),
            pltpu.VMEM((planes, strip + 16, width + 128), F32),
            pltpu.VMEM((planes, strip + 8, width + 128), F32),
            pltpu.VMEM((pc * strip, width), BF16),
            pltpu.VMEM((planes, colours, extc, width // 2), F32),
            pltpu.VMEM((planes, colours, ext1, width // 2), F32),
            pltpu.VMEM((planes, colours, ext2, width // 4), F32),
            pltpu.VMEM((max(pc * ext1, colours * strip, planes * ext0), width), BF16),
            pltpu.VMEM((max(pc * ext1, colours * strip, planes * ext0), width), BF16),
            pltpu.VMEM((pc * ext1, width // 2), F32),
            pltpu.VMEM((planes, colours, strip, width), F32),
            pltpu.VMEM((planes, strip, width), F32),
            pltpu.VMEM((strip, width), F32),
            pltpu.VMEM((2, strip, width), F32),
            pltpu.VMEM((strip, width), F32),
            pltpu.VMEM((planes, strip, width), F32),
            pltpu.VMEM((planes, ext0, width // 2), F32),
            pltpu.VMEM((planes * ext1, width // 4), F32),
            pltpu.VMEM((planes, ext1, width // 2), F32),
            pltpu.VMEM((planes, ext2, width // 4), F32),
            pltpu.VMEM((colours, ext1, width // 2), F32),
            pltpu.VMEM((colours, strip, width), F32),
            pltpu.VMEM((2, colours, strip, width), F32),
            dma((4, 2)), dma((4, 2)),
            dma((n_e,)), dma((2, n_e)), dma((n_e,)), dma((n_e,)),
            dma((n_j,)), dma((2, n_j)), dma((n_j,)), dma((n_j,)),
        ],
        compiler_params=pltpu.CompilerParams(
            collective_id=0, has_side_effects=True, vmem_limit_bytes=56 * 1024 * 1024
        ),
    )(samples, gain, *constants)


def solution(mesh):
    return jax.shard_map(
        functools.partial(on_device, mesh.shape["rows"], mesh.shape["gz"]),
        mesh=mesh,
        in_specs=(P("gz", None, "rows", None), P("gz")),
        out_specs=P(None, "rows", None),
        check_vma=False,
    )
```

```python
import functools

import jax
import jax.numpy as jnp
import ml_dtypes
import numpy as np
from jax import lax
from jax.experimental import pallas as pl
from jax.experimental.pallas import tpu as pltpu
from jax.sharding import PartitionSpec as P

MESH = pl.DeviceIdType.MESH
F32 = jnp.float32
BF16 = jnp.bfloat16
TAPS = (1 / 16, 4 / 16, 6 / 16, 4 / 16, 1 / 16)


def down_rows(rows_in):
    m = np.zeros((rows_in // 2, rows_in), np.float32)
    for i in range(rows_in // 2):
        for t, tap in enumerate(TAPS):
            if 0 <= 2 * i + t - 2 < rows_in:
                m[i, 2 * i + t - 2] = tap
    return m


def up_rows(rows_in, rows_out, first):
    m = np.zeros((rows_out, rows_in), np.float32)
    for i in range(rows_out):
        k = first + i // 2
        pairs = ((k - 1, 1 / 8), (k, 6 / 8), (k + 1, 1 / 8)) if i % 2 == 0 else ((k, 1 / 2), (k + 1, 1 / 2))
        for r, tap in pairs:
            if 0 <= r < rows_in:
                m[i, r] = tap
    return m


def down_block():
    m = np.zeros((768, 256), np.float32)
    for o in range(256):
        for t, tap in enumerate(TAPS):
            m[128 + 2 * o + t - 2, o] = tap
    return m


def up_block():
    m = np.zeros((512, 512), np.float32)
    for k in range(256):
        m[127 + k, 2 * k] = m[129 + k, 2 * k] = 1 / 8
        m[128 + k, 2 * k] = 6 / 8
        m[128 + k, 2 * k + 1] = m[129 + k, 2 * k + 1] = 1 / 2
    return m


def twice(count, matrix):
    diagonal = np.kron(np.eye(count, dtype=np.float32), matrix)
    return np.concatenate([diagonal, diagonal], axis=1)


def dot(a, b):
    return lax.dot_general(a, b, (((1,), (0,)), ((), ())), preferred_element_type=F32)


def terms(v):
    high = v.astype(BF16)
    return high, (v - high.astype(F32)).astype(BF16)


def folded(v, stacked):
    if not stacked:
        return v
    rows = v.shape[0] // 2
    return v[:rows] + v[rows:]


def col_down(source, matrix, width, put, stacked=True):
    for j in range(width // 512):
        first = 512 * j - 128
        low, high = max(0, first), min(width, first + 768)
        taps = matrix[low - first : high - first, :]
        put(256 * j, 256, folded(dot(source(low, high), taps), stacked))


def col_up(source, matrix, width, put):
    for j in range(width // 256):
        first = 256 * j - 128
        low, high = max(0, first), min(width, first + 512)
        taps = matrix[low - first : high - first, :]
        put(512 * j, 512, folded(dot(source(low, high), taps), True))


def row_apply(matrix, read, width, put):
    for low in range(0, width, 512):
        put(low, 512, dot(matrix, jnp.concatenate(terms(read(low, low + 512)), axis=0)))


def kernel(
    n_rows, n_gz, planes, colours, strip, width,
    x_hbm, gain_ref, *refs,
):
    constants, out_ref, rest = refs[:9], refs[9], refs[10:]
    copied, rest = rest[:9], rest[9:]
    body(n_rows, n_gz, planes, colours, strip, width, x_hbm, gain_ref, constants, copied, out_ref, *rest)


def body(
    n_rows, n_gz, planes, colours, strip, width, x_hbm, gain_ref, constants, copied, out_ref,
    x_ref, x_sem, const_sem,
    grey, sq, xb, cext, l1, l2, st, up2, detail, logit, lse, lse_in, lse_fin, w0, cw, cw2, w1, w2, c1, part, part_in,
    h_send, h_recv, e_send, e_recv, eo_send, eo_recv, j_send, j_recv, jo_send, jo_recv,
):
    pc = planes * colours
    half, quarter = strip // 2, strip // 4
    ext0, ext1, ext2 = strip + 32, half + 16, quarter + 8
    w_half, w_quarter = width // 2, width // 4
    r = lax.axis_index("rows")
    z = lax.axis_index("gz")
    has_up, has_down = r > 0, r < n_rows - 1
    upper, lower = jnp.maximum(r - 1, 0), jnp.minimum(r + 1, n_rows - 1)
    left = z < n_gz // 2
    inward = jnp.where(left, z + 1, z - 1)
    has_outer = jnp.logical_and(z > 0, z < n_gz - 1)
    outward = jnp.where(has_outer, jnp.where(left, z - 1, z + 1), z)
    is_mid = jnp.logical_or(z == n_gz // 2 - 1, z == n_gz // 2)
    slot = jnp.where(is_mid, 1, 0)
    not_mid = jnp.logical_not(is_mid)

    dcol_ref, ucol_ref, d1x_ref, d1w_ref, d2x_ref, d2w_ref, u2x_ref, u2b_ref, u1_ref = copied
    loads = [pltpu.make_async_copy(x_hbm.at[p], x_ref.at[p], x_sem.at[p]) for p in range(planes)]
    fetches = [pltpu.make_async_copy(a, b, const_sem.at[k]) for k, (a, b) in enumerate(zip(constants, copied))]
    for copy in loads + fetches:
        copy.start()

    barrier = pltpu.get_barrier_semaphore()

    def greet(cond, device):
        @pl.when(cond)
        def _():
            pl.semaphore_signal(barrier, inc=1, device_id=device, device_id_type=MESH)

    greet(has_up, {"rows": upper})
    greet(has_down, {"rows": lower})
    greet(has_outer, {"gz": outward})
    pl.semaphore_signal(barrier, inc=1, device_id={"gz": inward}, device_id_type=MESH)

    for p in range(planes):
        loads[p].wait()
        samples = [x_ref[p, c].astype(F32) for c in range(colours)]
        for c in range(colours):
            xb[pl.ds((p * colours + c) * strip, strip), :] = samples[c].astype(BF16)
        mixed = 0.299 * samples[0] + 0.587 * samples[1] + 0.114 * samples[2]
        grey[p, pl.ds(8, strip), :width] = mixed * (1.0 / 255.0)
        grey[p, pl.ds(8, strip), width:] = jnp.zeros((strip, 128), F32)

    @pl.when(jnp.logical_not(has_up))
    def _():
        grey[:, 0:8, :] = jnp.zeros((planes, 8, width + 128), F32)
        cext[:, :, 0:16, :] = jnp.zeros((planes, colours, 16, w_half), F32)
        cw[:, 0:16, :] = jnp.zeros((planes, 16, w_half), F32)

    @pl.when(jnp.logical_not(has_down))
    def _():
        grey[:, strip + 8 :, :] = jnp.zeros((planes, 8, width + 128), F32)
        cext[:, :, strip + 16 :, :] = jnp.zeros((planes, colours, 16, w_half), F32)
        cw[:, strip + 16 :, :] = jnp.zeros((planes, 16, w_half), F32)

    pl.semaphore_wait(
        barrier, 1 + has_up.astype(jnp.int32) + has_down.astype(jnp.int32) + has_outer.astype(jnp.int32)
    )

    def halo(kind, ref, lead, depth):
        def view(first):
            return ref.at[(slice(None),) * lead + (pl.ds(first, depth), slice(None))]

        def copies():
            up = pltpu.make_async_remote_copy(
                src_ref=view(depth), dst_ref=view(strip + depth),
                send_sem=h_send.at[kind, 0], recv_sem=h_recv.at[kind, 0],
                device_id={"rows": upper}, device_id_type=MESH,
            )
            down = pltpu.make_async_remote_copy(
                src_ref=view(strip), dst_ref=view(0),
                send_sem=h_send.at[kind, 1], recv_sem=h_recv.at[kind, 1],
                device_id={"rows": lower}, device_id_type=MESH,
            )
            return up, down

        def start():
            up, down = copies()
            pl.when(has_up)(up.start)
            pl.when(has_down)(down.start)

        def arrived():
            up, down = copies()
            pl.when(has_down)(up.wait_recv)
            pl.when(has_up)(down.wait_recv)

        def sent():
            up, down = copies()
            pl.when(has_up)(up.wait_send)
            pl.when(has_down)(down.wait_send)

        return start, arrived, sent

    def chain(own, arrive, final, send, recv, out_send, out_recv):
        def inner(view, k, s):
            return pltpu.make_async_remote_copy(
                src_ref=own.at[view], dst_ref=arrive.at[(s,) + view],
                send_sem=send.at[k], recv_sem=recv.at[s, k],
                device_id={"gz": inward}, device_id_type=MESH,
            )

        def outer(view, k):
            return pltpu.make_async_remote_copy(
                src_ref=final.at[view], dst_ref=final.at[view],
                send_sem=out_send.at[k], recv_sem=out_recv.at[k],
                device_id={"gz": outward}, device_id_type=MESH,
            )

        return inner, outer

    grey_start, grey_arrived, grey_sent = halo(0, grey, 1, 8)
    image_start, image_arrived, image_sent = halo(1, cext, 2, 16)
    weight_start, weight_arrived, weight_sent = halo(2, cw, 1, 16)
    e_inner, e_outer = chain(lse, lse_in, lse_fin, e_send, e_recv, eo_send, eo_recv)
    j_inner, j_outer = chain(part, part_in, out_ref, j_send, j_recv, jo_send, jo_recv)

    grey_start()
    for copy in fetches:
        copy.wait()

    def put_c(low, count, v):
        cext[:, :, pl.ds(16, strip), low : low + count] = (v * (1.0 / 255.0)).reshape(planes, colours, strip, count)

    col_down(lambda a, b: xb[:, a:b], dcol_ref, width, put_c, False)
    image_start()

    padded = width + 128
    e_chunks = [(pl.ds(8 * t, 8), slice(None)) for t in range(strip // 8)]

    def square(p, i):
        line = lax.broadcasted_iota(jnp.int32, (8, padded), 0) + (r * strip - 4 + 8 * i)
        column = lax.broadcasted_iota(jnp.int32, (8, padded), 1)
        inside = (line >= 0) & (line < strip * n_rows) & (column < width)
        centre = grey[p, pl.ds(4 + 8 * i, 8), :]
        lap = 4.0 * centre - grey[p, pl.ds(3 + 8 * i, 8), :] - grey[p, pl.ds(5 + 8 * i, 8), :]
        lap = lap - pltpu.roll(centre, 1, 1) - pltpu.roll(centre, padded - 1, 1)
        lap = jnp.where(inside, lap, 0.0)
        sq[p, pl.ds(8 * i, 8), :] = lap * lap

    def merge(a, b):
        return jnp.maximum(a, b) + jnp.log(1.0 + jnp.exp(-jnp.abs(a - b)))

    def clarity(t):
        rows = pl.ds(8 * t, 8)
        top = None
        for p in range(planes):
            total = sq[p, rows, :]
            for k in range(1, 9):
                total = total + sq[p, pl.ds(8 * t + k, 8), :]
            two = total + pltpu.roll(total, 1, 1)
            four = two + pltpu.roll(two, 2, 1)
            eight = four + pltpu.roll(four, 4, 1)
            nine = eight + pltpu.roll(total, 8, 1)
            energy = pltpu.roll(nine, padded - 4, 1)
            scaled = energy[:, :width] * gain_ref[p]
            logit[p, rows, :] = scaled
            top = scaled if top is None else merge(top, scaled)
        lse[rows, :] = top

        @pl.when(jnp.logical_not(has_outer))
        def _():
            e_inner(e_chunks[t], t, slot).start()

    last = strip // 8
    for i in range(1, last):
        for p in range(planes):
            square(p, i)
    for t in range(1, last - 1):
        clarity(t)

    grey_arrived()
    for p in range(planes):
        square(p, 0)
        square(p, last)
    e_order = list(range(1, last - 1)) + sorted({0, last - 1})
    for t in e_order[last - 2 :]:
        clarity(t)

    @pl.when(has_outer)
    def _():
        for k in e_order:
            view = e_chunks[k]
            e_inner(view, k, 0).wait_recv()
            lse[view] = merge(lse[view], lse_in[(0,) + view])
            e_inner(view, k, slot).start()

    image_arrived()

    def edge_mask(rows_ext, margin, rows_own):
        row = lax.broadcasted_iota(jnp.int32, (rows_ext, 512), 0) + (r * rows_own - margin)
        return ((row >= 0) & (row < rows_own * n_rows)).astype(F32)[None]

    mask1 = edge_mask(ext1, 8, half)
    mask2 = edge_mask(ext2, 4, quarter)
    for p in range(planes):
        def put_l1(low, count, v):
            l1[p, :, :, low : low + count] = v.reshape(colours, ext1, count) * mask1

        row_apply(d1x_ref[...], lambda a, b: cext[p, :, :, a:b].reshape(colours * ext0, b - a), w_half, put_l1)

    def stage(rows, low, count, v, base=0):
        size = v.shape[0]
        high, rest = terms(v)
        st[pl.ds(base, size), low : low + count] = high
        st[pl.ds(rows + base, size), low : low + count] = rest

    def staged(rows):
        return lambda a, b: st[0 : 2 * rows, a:b]

    full = colours * strip
    for p in range(planes):
        row_apply(
            u1_ref[...], lambda a, b: l1[p, :, :, a:b].reshape(colours * ext1, b - a), w_half,
            functools.partial(stage, planes * full, base=p * full),
        )

    def put_detail(low, count, v):
        samples = xb[:, low : low + count].astype(F32)
        detail[:, :, :, low : low + count] = (samples * (1.0 / 255.0) - v).reshape(planes, colours, strip, count)

    col_up(staged(planes * full), ucol_ref, w_half, put_detail)

    for k in e_order:
        view = e_chunks[k]

        @pl.when(is_mid)
        def _():
            e_inner(view, k, 1).wait_recv()
            lse_fin[view] = merge(lse[view], lse_in[(1,) + view])

        @pl.when(not_mid)
        def _():
            e_outer(view, k).wait_recv()

        pl.when(has_outer)(e_outer(view, k).start)
        for p in range(planes):
            w0[(p,) + view] = jnp.exp(logit[(p,) + view] - lse_fin[view])

    own_rows = planes * strip
    for low in range(0, width, 512):
        stage(own_rows, low, 512, w0[:, :, low : low + 512].reshape(own_rows, 512))

    def put_cw(low, count, v):
        cw[:, pl.ds(16, strip), low : low + count] = v.reshape(planes, strip, count)

    col_down(staged(own_rows), dcol_ref, width, put_cw)
    weight_start()

    for low in range(0, width, 512):
        for c in range(colours):
            acc = w0[0, :, low : low + 512] * detail[0, c, :, low : low + 512]
            for p in range(1, planes):
                acc = acc + w0[p, :, low : low + 512] * detail[p, c, :, low : low + 512]
            part[c, :, low : low + 512] = acc

    rows1 = pc * ext1
    for low in range(0, w_half, 512):
        stage(rows1, low, 512, l1[:, :, :, low : low + 512].reshape(rows1, 512))

    def put_c2(low, count, v):
        up2[:, low : low + count] = v

    col_down(staged(rows1), dcol_ref, w_half, put_c2)

    def put_l2(low, count, v):
        l2[:, :, :, low : low + count] = (v.reshape(pc, ext2, count) * mask2).reshape(planes, colours, ext2, count)

    row_apply(d2x_ref[...], lambda a, b: up2[:, a:b], w_quarter, put_l2)
    row_apply(
        u2x_ref[...], lambda a, b: l2[:, :, :, a:b].reshape(pc * ext2, b - a), w_quarter,
        functools.partial(stage, rows1),
    )

    def put_up2(low, count, v):
        up2[:, low : low + count] = v

    col_up(staged(rows1), ucol_ref, w_quarter, put_up2)

    weight_arrived()
    w_rows = planes * ext0

    def put_w1(low, count, v):
        w1[:, :, low : low + count] = v.reshape(planes, ext1, count) * mask1

    row_apply(d1w_ref[...], lambda a, b: cw[:, :, a:b].reshape(w_rows, b - a), w_half, put_w1)
    w1_rows = planes * ext1
    for low in range(0, w_half, 512):
        stage(w1_rows, low, 512, w1[:, :, low : low + 512].reshape(w1_rows, 512))

    def put_cw2(low, count, v):
        cw2[:, low : low + count] = v

    col_down(staged(w1_rows), dcol_ref, w_half, put_cw2)

    def put_w2(low, count, v):
        w2[:, :, low : low + count] = v.reshape(planes, ext2, count) * mask2

    row_apply(d2w_ref[...], lambda a, b: cw2[:, a:b], w_quarter, put_w2)

    def read_b2(a, b):
        acc = w2[0, :, a:b][None] * l2[0, :, :, a:b]
        for p in range(1, planes):
            acc = acc + w2[p, :, a:b][None] * l2[p, :, :, a:b]
        return acc.reshape(colours * ext2, b - a)

    rows_c1 = colours * ext1
    row_apply(u2b_ref[...], read_b2, w_quarter, functools.partial(stage, rows_c1))

    def put_c1(low, count, v):
        acc = v.reshape(colours, ext1, count)
        for p in range(planes):
            first = p * rows_c1
            coarse = up2[pl.ds(first, rows_c1), low : low + count].reshape(colours, ext1, count)
            acc = acc + w1[p, :, low : low + count][None] * (l1[p, :, :, low : low + count] - coarse)
        c1[:, :, low : low + count] = acc * mask1

    col_up(staged(rows_c1), ucol_ref, w_quarter, put_c1)

    row_apply(
        u1_ref[...], lambda a, b: c1[:, :, a:b].reshape(rows_c1, b - a), w_half, functools.partial(stage, full)
    )

    j_chunks = [(c, slice(None), slice(low, low + 512)) for low in range(0, width, 512) for c in range(colours)]

    def into(k):
        view = j_chunks[k]

        @pl.when(has_outer)
        def _():
            j_inner(view, k, 0).wait_recv()
            part[view] = part[view] + part_in[(0,) + view]
            j_inner(view, k, slot).start()

    def put_part(low, count, v):
        part[:, :, low : low + count] += v.reshape(colours, strip, count)

        @pl.when(jnp.logical_not(has_outer))
        def _():
            for c in range(colours):
                k = low // count * colours + c
                j_inner(j_chunks[k], k, slot).start()

        for k in range(max(0, low // count - 1) * colours, low // count * colours):
            into(k)

    col_up(staged(full), ucol_ref, w_half, put_part)

    def back(k):
        view = j_chunks[k]

        @pl.when(is_mid)
        def _():
            j_inner(view, k, 1).wait_recv()
            out_ref[view] = part[view] + part_in[(1,) + view]

        @pl.when(not_mid)
        def _():
            j_outer(view, k).wait_recv()

        pl.when(has_outer)(j_outer(view, k).start)

    for k in range(len(j_chunks)):
        if k < colours:
            into(len(j_chunks) - colours + k)
        back(k)

    grey_sent()
    image_sent()
    weight_sent()
    for k, view in enumerate(e_chunks):
        e_inner(view, k, slot).wait_send()
        pl.when(has_outer)(e_outer(view, k).wait_send)
    for k, view in enumerate(j_chunks):
        j_inner(view, k, slot).wait_send()
        pl.when(has_outer)(j_outer(view, k).wait_send)


def on_device(n_rows, n_gz, samples, gain):
    planes, colours, strip, width = samples.shape
    pc = planes * colours
    half, quarter = strip // 2, strip // 4
    ext0, ext1, ext2 = strip + 32, half + 16, quarter + 8
    d1, d2 = down_rows(ext0), down_rows(ext1)
    u2, u1 = up_rows(ext2, ext1, 0), up_rows(ext1, strip, 8)
    constants = [
        down_block(), up_block(), twice(colours, d1), twice(planes, d1), twice(pc, d2), twice(planes, d2),
        twice(pc, u2), twice(colours, u2), twice(colours, u1),
    ]
    constants = [jnp.asarray(c.astype(ml_dtypes.bfloat16)) for c in constants]
    n_e, n_j = strip // 8, colours * width // 512
    dma = pltpu.SemaphoreType.DMA
    vmem = pl.BlockSpec(memory_space=pltpu.VMEM)
    hbm = pl.BlockSpec(memory_space=pltpu.HBM)
    return pl.pallas_call(
        functools.partial(kernel, n_rows, n_gz, planes, colours, strip, width),
        out_shape=jax.ShapeDtypeStruct((colours, strip, width), F32),
        in_specs=[hbm, pl.BlockSpec(memory_space=pltpu.SMEM)] + [hbm] * len(constants),
        out_specs=vmem,
        scratch_shapes=[pltpu.VMEM(c.shape, c.dtype) for c in constants] + [
            pltpu.VMEM(samples.shape, samples.dtype),
            dma((planes,)), dma((len(constants),)),
            pltpu.VMEM((planes, strip + 16, width + 128), F32),
            pltpu.VMEM((planes, strip + 8, width + 128), F32),
            pltpu.VMEM((pc * strip, width), BF16),
            pltpu.VMEM((planes, colours, ext0, width // 2), F32),
            pltpu.VMEM((planes, colours, ext1, width // 2), F32),
            pltpu.VMEM((planes, colours, ext2, width // 4), F32),
            pltpu.VMEM((2 * max(pc * ext1, pc * strip), width), BF16),
            pltpu.VMEM((pc * ext1, width // 2), F32),
            pltpu.VMEM((planes, colours, strip, width), F32),
            pltpu.VMEM((planes, strip, width), F32),
            pltpu.VMEM((strip, width), F32),
            pltpu.VMEM((2, strip, width), F32),
            pltpu.VMEM((strip, width), F32),
            pltpu.VMEM((planes, strip, width), F32),
            pltpu.VMEM((planes, ext0, width // 2), F32),
            pltpu.VMEM((planes * ext1, width // 4), F32),
            pltpu.VMEM((planes, ext1, width // 2), F32),
            pltpu.VMEM((planes, ext2, width // 4), F32),
            pltpu.VMEM((colours, ext1, width // 2), F32),
            pltpu.VMEM((colours, strip, width), F32),
            pltpu.VMEM((2, colours, strip, width), F32),
            dma((3, 2)), dma((3, 2)),
            dma((n_e,)), dma((2, n_e)), dma((n_e,)), dma((n_e,)),
            dma((n_j,)), dma((2, n_j)), dma((n_j,)), dma((n_j,)),
        ],
        compiler_params=pltpu.CompilerParams(
            collective_id=0, has_side_effects=True, vmem_limit_bytes=56 * 1024 * 1024
        ),
    )(samples, gain, *constants)


def solution(mesh):
    return jax.shard_map(
        functools.partial(on_device, mesh.shape["rows"], mesh.shape["gz"]),
        mesh=mesh,
        in_specs=(P("gz", None, "rows", None), P("gz")),
        out_specs=P(None, "rows", None),
        check_vma=False,
    )
```

```python
import functools

import jax
import jax.numpy as jnp
import ml_dtypes
import numpy as np
from jax import lax
from jax.experimental import pallas as pl
from jax.experimental.pallas import tpu as pltpu
from jax.sharding import PartitionSpec as P

MESH = pl.DeviceIdType.MESH
F32 = jnp.float32
BF16 = jnp.bfloat16
TAPS = (1 / 16, 4 / 16, 6 / 16, 4 / 16, 1 / 16)


def down_rows(rows_in):
    m = np.zeros((rows_in // 2, rows_in), np.float32)
    for i in range(rows_in // 2):
        for t, tap in enumerate(TAPS):
            if 0 <= 2 * i + t - 2 < rows_in:
                m[i, 2 * i + t - 2] = tap
    return m


def up_rows(rows_in, rows_out, first):
    m = np.zeros((rows_out, rows_in), np.float32)
    for i in range(rows_out):
        k = first + i // 2
        pairs = ((k - 1, 1 / 8), (k, 6 / 8), (k + 1, 1 / 8)) if i % 2 == 0 else ((k, 1 / 2), (k + 1, 1 / 2))
        for r, tap in pairs:
            if 0 <= r < rows_in:
                m[i, r] = tap
    return m


def down_block():
    m = np.zeros((768, 256), np.float32)
    for o in range(256):
        for t, tap in enumerate(TAPS):
            m[128 + 2 * o + t - 2, o] = tap
    return m


def up_block():
    m = np.zeros((512, 512), np.float32)
    for k in range(256):
        m[127 + k, 2 * k] = m[129 + k, 2 * k] = 1 / 8
        m[128 + k, 2 * k] = 6 / 8
        m[128 + k, 2 * k + 1] = m[129 + k, 2 * k + 1] = 1 / 2
    return m


def twice(count, matrix):
    diagonal = np.kron(np.eye(count, dtype=np.float32), matrix)
    return np.concatenate([diagonal, diagonal], axis=1)


def dot(a, b):
    return lax.dot_general(a, b, (((1,), (0,)), ((), ())), preferred_element_type=F32)


def terms(v):
    high = v.astype(BF16)
    return high, (v - high.astype(F32)).astype(BF16)


def folded(v, stacked):
    if not stacked:
        return v
    rows = v.shape[0] // 2
    return v[:rows] + v[rows:]


def col_down(source, matrix, width, put, stacked=True):
    for j in range(width // 512):
        first = 512 * j - 128
        low, high = max(0, first), min(width, first + 768)
        taps = matrix[low - first : high - first, :]
        put(256 * j, 256, folded(dot(source(low, high), taps), stacked))


def col_up(source, matrix, width, put):
    for j in range(width // 256):
        first = 256 * j - 128
        low, high = max(0, first), min(width, first + 512)
        taps = matrix[low - first : high - first, :]
        put(512 * j, 512, folded(dot(source(low, high), taps), True))


def row_apply(matrix, read, width, put):
    for low in range(0, width, 512):
        put(low, 512, dot(matrix, jnp.concatenate(terms(read(low, low + 512)), axis=0)))


def kernel(
    n_rows, n_gz, planes, colours, strip, width,
    x_hbm, gain_ref, *refs,
):
    constants, out_ref, rest = refs[:9], refs[9], refs[10:]
    copied, rest = rest[:9], rest[9:]
    body(n_rows, n_gz, planes, colours, strip, width, x_hbm, gain_ref, constants, copied, out_ref, *rest)


def body(
    n_rows, n_gz, planes, colours, strip, width, x_hbm, gain_ref, constants, copied, out_ref,
    x_ref, x_sem, const_sem,
    grey, sq, xb, cext, l1, l2, st, up2, detail, logit, lse, lse_in, lse_fin, w0, cw, cw2, w1, w2, c1, part, part_in,
    h_send, h_recv, e_send, e_recv, eo_send, eo_recv, j_send, j_recv, jo_send, jo_recv,
):
    pc = planes * colours
    half, quarter = strip // 2, strip // 4
    ext0, ext1, ext2 = strip + 32, half + 16, quarter + 8
    w_half, w_quarter = width // 2, width // 4
    r = lax.axis_index("rows")
    z = lax.axis_index("gz")
    has_up, has_down = r > 0, r < n_rows - 1
    upper, lower = jnp.maximum(r - 1, 0), jnp.minimum(r + 1, n_rows - 1)
    left = z < n_gz // 2
    inward = jnp.where(left, z + 1, z - 1)
    has_outer = jnp.logical_and(z > 0, z < n_gz - 1)
    outward = jnp.where(has_outer, jnp.where(left, z - 1, z + 1), z)
    is_mid = jnp.logical_or(z == n_gz // 2 - 1, z == n_gz // 2)
    slot = jnp.where(is_mid, 1, 0)
    not_mid = jnp.logical_not(is_mid)

    dcol_ref, ucol_ref, d1x_ref, d1w_ref, d2x_ref, d2w_ref, u2x_ref, u2b_ref, u1_ref = copied
    loads = [pltpu.make_async_copy(x_hbm.at[p], x_ref.at[p], x_sem.at[p]) for p in range(planes)]
    fetches = [pltpu.make_async_copy(a, b, const_sem.at[k]) for k, (a, b) in enumerate(zip(constants, copied))]
    for copy in loads + fetches:
        copy.start()

    barrier = pltpu.get_barrier_semaphore()

    def greet(cond, device):
        @pl.when(cond)
        def _():
            pl.semaphore_signal(barrier, inc=1, device_id=device, device_id_type=MESH)

    greet(has_up, {"rows": upper})
    greet(has_down, {"rows": lower})
    greet(has_outer, {"gz": outward})
    pl.semaphore_signal(barrier, inc=1, device_id={"gz": inward}, device_id_type=MESH)

    for p in range(planes):
        loads[p].wait()
        samples = [x_ref[p, c].astype(F32) for c in range(colours)]
        for c in range(colours):
            xb[pl.ds((p * colours + c) * strip, strip), :] = samples[c].astype(BF16)
        mixed = 0.299 * samples[0] + 0.587 * samples[1] + 0.114 * samples[2]
        grey[p, pl.ds(8, strip), :width] = mixed * (1.0 / 255.0)
        grey[p, pl.ds(8, strip), width:] = jnp.zeros((strip, 128), F32)

    @pl.when(jnp.logical_not(has_up))
    def _():
        grey[:, 0:8, :] = jnp.zeros((planes, 8, width + 128), F32)
        cext[:, :, 0:16, :] = jnp.zeros((planes, colours, 16, w_half), F32)
        cw[:, 0:16, :] = jnp.zeros((planes, 16, w_half), F32)

    @pl.when(jnp.logical_not(has_down))
    def _():
        grey[:, strip + 8 :, :] = jnp.zeros((planes, 8, width + 128), F32)
        cext[:, :, strip + 16 :, :] = jnp.zeros((planes, colours, 16, w_half), F32)
        cw[:, strip + 16 :, :] = jnp.zeros((planes, 16, w_half), F32)

    pl.semaphore_wait(
        barrier, 1 + has_up.astype(jnp.int32) + has_down.astype(jnp.int32) + has_outer.astype(jnp.int32)
    )

    def halo(kind, ref, lead, depth):
        def view(first):
            return ref.at[(slice(None),) * lead + (pl.ds(first, depth), slice(None))]

        def copies():
            up = pltpu.make_async_remote_copy(
                src_ref=view(depth), dst_ref=view(strip + depth),
                send_sem=h_send.at[kind, 0], recv_sem=h_recv.at[kind, 0],
                device_id={"rows": upper}, device_id_type=MESH,
            )
            down = pltpu.make_async_remote_copy(
                src_ref=view(strip), dst_ref=view(0),
                send_sem=h_send.at[kind, 1], recv_sem=h_recv.at[kind, 1],
                device_id={"rows": lower}, device_id_type=MESH,
            )
            return up, down

        def start():
            up, down = copies()
            pl.when(has_up)(up.start)
            pl.when(has_down)(down.start)

        def arrived():
            up, down = copies()
            pl.when(has_down)(up.wait_recv)
            pl.when(has_up)(down.wait_recv)

        def sent():
            up, down = copies()
            pl.when(has_up)(up.wait_send)
            pl.when(has_down)(down.wait_send)

        return start, arrived, sent

    def chain(own, arrive, final, send, recv, out_send, out_recv):
        def inner(view, k, s):
            return pltpu.make_async_remote_copy(
                src_ref=own.at[view], dst_ref=arrive.at[(s,) + view],
                send_sem=send.at[k], recv_sem=recv.at[s, k],
                device_id={"gz": inward}, device_id_type=MESH,
            )

        def outer(view, k):
            return pltpu.make_async_remote_copy(
                src_ref=final.at[view], dst_ref=final.at[view],
                send_sem=out_send.at[k], recv_sem=out_recv.at[k],
                device_id={"gz": outward}, device_id_type=MESH,
            )

        return inner, outer

    grey_start, grey_arrived, grey_sent = halo(0, grey, 1, 8)
    image_start, image_arrived, image_sent = halo(1, cext, 2, 16)
    weight_start, weight_arrived, weight_sent = halo(2, cw, 1, 16)
    e_inner, e_outer = chain(lse, lse_in, lse_fin, e_send, e_recv, eo_send, eo_recv)
    j_inner, j_outer = chain(part, part_in, out_ref, j_send, j_recv, jo_send, jo_recv)

    grey_start()
    for copy in fetches:
        copy.wait()

    def put_c(low, count, v):
        cext[:, :, pl.ds(16, strip), low : low + count] = (v * (1.0 / 255.0)).reshape(planes, colours, strip, count)

    col_down(lambda a, b: xb[:, a:b], dcol_ref, width, put_c, False)
    image_start()

    padded = width + 128
    e_chunks = [(pl.ds(8 * t, 8), slice(None)) for t in range(strip // 8)]

    def square(p, i):
        line = lax.broadcasted_iota(jnp.int32, (8, padded), 0) + (r * strip - 4 + 8 * i)
        column = lax.broadcasted_iota(jnp.int32, (8, padded), 1)
        inside = (line >= 0) & (line < strip * n_rows) & (column < width)
        centre = grey[p, pl.ds(4 + 8 * i, 8), :]
        lap = 4.0 * centre - grey[p, pl.ds(3 + 8 * i, 8), :] - grey[p, pl.ds(5 + 8 * i, 8), :]
        lap = lap - pltpu.roll(centre, 1, 1) - pltpu.roll(centre, padded - 1, 1)
        lap = jnp.where(inside, lap, 0.0)
        sq[p, pl.ds(8 * i, 8), :] = lap * lap

    def merge(a, b):
        return jnp.maximum(a, b) + jnp.log(1.0 + jnp.exp(-jnp.abs(a - b)))

    def clarity(t):
        rows = pl.ds(8 * t, 8)
        top = None
        for p in range(planes):
            total = sq[p, rows, :]
            for k in range(1, 9):
                total = total + sq[p, pl.ds(8 * t + k, 8), :]
            two = total + pltpu.roll(total, 1, 1)
            four = two + pltpu.roll(two, 2, 1)
            eight = four + pltpu.roll(four, 4, 1)
            nine = eight + pltpu.roll(total, 8, 1)
            energy = pltpu.roll(nine, padded - 4, 1)
            scaled = energy[:, :width] * gain_ref[p]
            logit[p, rows, :] = scaled
            top = scaled if top is None else merge(top, scaled)
        lse[rows, :] = top

        @pl.when(jnp.logical_not(has_outer))
        def _():
            e_inner(e_chunks[t], t, slot).start()

    last = strip // 8
    for i in range(1, last):
        for p in range(planes):
            square(p, i)
    for t in range(1, last - 1):
        clarity(t)

    grey_arrived()
    for p in range(planes):
        square(p, 0)
        square(p, last)
    e_order = list(range(1, last - 1)) + sorted({0, last - 1})
    for t in e_order[last - 2 :]:
        clarity(t)

    @pl.when(has_outer)
    def _():
        for k in e_order:
            view = e_chunks[k]
            e_inner(view, k, 0).wait_recv()
            lse[view] = merge(lse[view], lse_in[(0,) + view])
            e_inner(view, k, slot).start()

    @pl.when(is_mid)
    def _():
        for k in e_order:
            view = e_chunks[k]
            e_inner(view, k, 1).wait_recv()
            lse_fin[view] = merge(lse[view], lse_in[(1,) + view])
            pl.when(has_outer)(e_outer(view, k).start)

    image_arrived()

    def edge_mask(rows_ext, margin, rows_own):
        row = lax.broadcasted_iota(jnp.int32, (rows_ext, 512), 0) + (r * rows_own - margin)
        return ((row >= 0) & (row < rows_own * n_rows)).astype(F32)[None]

    mask1 = edge_mask(ext1, 8, half)
    mask2 = edge_mask(ext2, 4, quarter)
    for p in range(planes):
        def put_l1(low, count, v):
            l1[p, :, :, low : low + count] = v.reshape(colours, ext1, count) * mask1

        row_apply(d1x_ref[...], lambda a, b: cext[p, :, :, a:b].reshape(colours * ext0, b - a), w_half, put_l1)

    def stage(rows, low, count, v, base=0):
        size = v.shape[0]
        high, rest = terms(v)
        st[pl.ds(base, size), low : low + count] = high
        st[pl.ds(rows + base, size), low : low + count] = rest

    def staged(rows):
        return lambda a, b: st[0 : 2 * rows, a:b]

    full = colours * strip
    for p in range(planes):
        row_apply(
            u1_ref[...], lambda a, b: l1[p, :, :, a:b].reshape(colours * ext1, b - a), w_half,
            functools.partial(stage, planes * full, base=p * full),
        )

    def put_detail(low, count, v):
        samples = xb[:, low : low + count].astype(F32)
        detail[:, :, :, low : low + count] = (samples * (1.0 / 255.0) - v).reshape(planes, colours, strip, count)

    col_up(staged(planes * full), ucol_ref, w_half, put_detail)

    @pl.when(not_mid)
    def _():
        for k in e_order:
            e_outer(e_chunks[k], k).wait_recv()
            pl.when(has_outer)(e_outer(e_chunks[k], k).start)

    for t in range(strip // 8):
        view = e_chunks[t]
        for p in range(planes):
            w0[(p,) + view] = jnp.exp(logit[(p,) + view] - lse_fin[view])

    own_rows = planes * strip
    for low in range(0, width, 512):
        stage(own_rows, low, 512, w0[:, :, low : low + 512].reshape(own_rows, 512))

    def put_cw(low, count, v):
        cw[:, pl.ds(16, strip), low : low + count] = v.reshape(planes, strip, count)

    col_down(staged(own_rows), dcol_ref, width, put_cw)
    weight_start()

    for low in range(0, width, 512):
        for c in range(colours):
            acc = w0[0, :, low : low + 512] * detail[0, c, :, low : low + 512]
            for p in range(1, planes):
                acc = acc + w0[p, :, low : low + 512] * detail[p, c, :, low : low + 512]
            part[c, :, low : low + 512] = acc

    rows1 = pc * ext1
    for low in range(0, w_half, 512):
        stage(rows1, low, 512, l1[:, :, :, low : low + 512].reshape(rows1, 512))

    def put_c2(low, count, v):
        up2[:, low : low + count] = v

    col_down(staged(rows1), dcol_ref, w_half, put_c2)

    def put_l2(low, count, v):
        l2[:, :, :, low : low + count] = (v.reshape(pc, ext2, count) * mask2).reshape(planes, colours, ext2, count)

    row_apply(d2x_ref[...], lambda a, b: up2[:, a:b], w_quarter, put_l2)
    row_apply(
        u2x_ref[...], lambda a, b: l2[:, :, :, a:b].reshape(pc * ext2, b - a), w_quarter,
        functools.partial(stage, rows1),
    )

    def put_up2(low, count, v):
        up2[:, low : low + count] = v

    col_up(staged(rows1), ucol_ref, w_quarter, put_up2)

    weight_arrived()
    w_rows = planes * ext0

    def put_w1(low, count, v):
        w1[:, :, low : low + count] = v.reshape(planes, ext1, count) * mask1

    row_apply(d1w_ref[...], lambda a, b: cw[:, :, a:b].reshape(w_rows, b - a), w_half, put_w1)
    w1_rows = planes * ext1
    for low in range(0, w_half, 512):
        stage(w1_rows, low, 512, w1[:, :, low : low + 512].reshape(w1_rows, 512))

    def put_cw2(low, count, v):
        cw2[:, low : low + count] = v

    col_down(staged(w1_rows), dcol_ref, w_half, put_cw2)

    def put_w2(low, count, v):
        w2[:, :, low : low + count] = v.reshape(planes, ext2, count) * mask2

    row_apply(d2w_ref[...], lambda a, b: cw2[:, a:b], w_quarter, put_w2)

    def read_b2(a, b):
        acc = w2[0, :, a:b][None] * l2[0, :, :, a:b]
        for p in range(1, planes):
            acc = acc + w2[p, :, a:b][None] * l2[p, :, :, a:b]
        return acc.reshape(colours * ext2, b - a)

    rows_c1 = colours * ext1
    row_apply(u2b_ref[...], read_b2, w_quarter, functools.partial(stage, rows_c1))

    def put_c1(low, count, v):
        acc = v.reshape(colours, ext1, count)
        for p in range(planes):
            first = p * rows_c1
            coarse = up2[pl.ds(first, rows_c1), low : low + count].reshape(colours, ext1, count)
            acc = acc + w1[p, :, low : low + count][None] * (l1[p, :, :, low : low + count] - coarse)
        c1[:, :, low : low + count] = acc * mask1

    col_up(staged(rows_c1), ucol_ref, w_quarter, put_c1)

    row_apply(
        u1_ref[...], lambda a, b: c1[:, :, a:b].reshape(rows_c1, b - a), w_half, functools.partial(stage, full)
    )

    j_chunks = [(c, slice(None), slice(low, low + 512)) for low in range(0, width, 512) for c in range(colours)]

    def into(k):
        view = j_chunks[k]

        @pl.when(has_outer)
        def _():
            j_inner(view, k, 0).wait_recv()
            part[view] = part[view] + part_in[(0,) + view]
            j_inner(view, k, slot).start()

    lag = 3

    def step(k):
        if k < len(j_chunks):
            into(k)
        if k >= lag:
            view = j_chunks[k - lag]

            @pl.when(is_mid)
            def _():
                j_inner(view, k - lag, 1).wait_recv()
                out_ref[view] = part[view] + part_in[(1,) + view]
                pl.when(has_outer)(j_outer(view, k - lag).start)

    def put_part(low, count, v):
        part[:, :, low : low + count] += v.reshape(colours, strip, count)

        @pl.when(jnp.logical_not(has_outer))
        def _():
            for c in range(colours):
                k = low // count * colours + c
                j_inner(j_chunks[k], k, slot).start()

        for k in range(max(0, low // count - 1) * colours, low // count * colours):
            step(k)

    col_up(staged(full), ucol_ref, w_half, put_part)

    for k in range(len(j_chunks) - colours, len(j_chunks) + lag):
        step(k)

    @pl.when(not_mid)
    def _():
        for k, view in enumerate(j_chunks):
            j_outer(view, k).wait_recv()
            pl.when(has_outer)(j_outer(view, k).start)

    grey_sent()
    image_sent()
    weight_sent()
    for k, view in enumerate(e_chunks):
        e_inner(view, k, slot).wait_send()
        pl.when(has_outer)(e_outer(view, k).wait_send)
    for k, view in enumerate(j_chunks):
        j_inner(view, k, slot).wait_send()
        pl.when(has_outer)(j_outer(view, k).wait_send)


def on_device(n_rows, n_gz, samples, gain):
    planes, colours, strip, width = samples.shape
    pc = planes * colours
    half, quarter = strip // 2, strip // 4
    ext0, ext1, ext2 = strip + 32, half + 16, quarter + 8
    d1, d2 = down_rows(ext0), down_rows(ext1)
    u2, u1 = up_rows(ext2, ext1, 0), up_rows(ext1, strip, 8)
    constants = [
        down_block(), up_block(), twice(colours, d1), twice(planes, d1), twice(pc, d2), twice(planes, d2),
        twice(pc, u2), twice(colours, u2), twice(colours, u1),
    ]
    constants = [jnp.asarray(c.astype(ml_dtypes.bfloat16)) for c in constants]
    n_e, n_j = strip // 8, colours * width // 512
    dma = pltpu.SemaphoreType.DMA
    vmem = pl.BlockSpec(memory_space=pltpu.VMEM)
    hbm = pl.BlockSpec(memory_space=pltpu.HBM)
    return pl.pallas_call(
        functools.partial(kernel, n_rows, n_gz, planes, colours, strip, width),
        out_shape=jax.ShapeDtypeStruct((colours, strip, width), F32),
        in_specs=[hbm, pl.BlockSpec(memory_space=pltpu.SMEM)] + [hbm] * len(constants),
        out_specs=vmem,
        scratch_shapes=[pltpu.VMEM(c.shape, c.dtype) for c in constants] + [
            pltpu.VMEM(samples.shape, samples.dtype),
            dma((planes,)), dma((len(constants),)),
            pltpu.VMEM((planes, strip + 16, width + 128), F32),
            pltpu.VMEM((planes, strip + 8, width + 128), F32),
            pltpu.VMEM((pc * strip, width), BF16),
            pltpu.VMEM((planes, colours, ext0, width // 2), F32),
            pltpu.VMEM((planes, colours, ext1, width // 2), F32),
            pltpu.VMEM((planes, colours, ext2, width // 4), F32),
            pltpu.VMEM((2 * max(pc * ext1, pc * strip), width), BF16),
            pltpu.VMEM((pc * ext1, width // 2), F32),
            pltpu.VMEM((planes, colours, strip, width), F32),
            pltpu.VMEM((planes, strip, width), F32),
            pltpu.VMEM((strip, width), F32),
            pltpu.VMEM((2, strip, width), F32),
            pltpu.VMEM((strip, width), F32),
            pltpu.VMEM((planes, strip, width), F32),
            pltpu.VMEM((planes, ext0, width // 2), F32),
            pltpu.VMEM((planes * ext1, width // 4), F32),
            pltpu.VMEM((planes, ext1, width // 2), F32),
            pltpu.VMEM((planes, ext2, width // 4), F32),
            pltpu.VMEM((colours, ext1, width // 2), F32),
            pltpu.VMEM((colours, strip, width), F32),
            pltpu.VMEM((2, colours, strip, width), F32),
            dma((3, 2)), dma((3, 2)),
            dma((n_e,)), dma((2, n_e)), dma((n_e,)), dma((n_e,)),
            dma((n_j,)), dma((2, n_j)), dma((n_j,)), dma((n_j,)),
        ],
        compiler_params=pltpu.CompilerParams(
            collective_id=0, has_side_effects=True, vmem_limit_bytes=56 * 1024 * 1024
        ),
    )(samples, gain, *constants)


def solution(mesh):
    return jax.shard_map(
        functools.partial(on_device, mesh.shape["rows"], mesh.shape["gz"]),
        mesh=mesh,
        in_specs=(P("gz", None, "rows", None), P("gz")),
        out_specs=P(None, "rows", None),
        check_vma=False,
    )
```

```python
import functools

import jax
import jax.numpy as jnp
import ml_dtypes
import numpy as np
from jax import lax
from jax.experimental import pallas as pl
from jax.experimental.pallas import tpu as pltpu
from jax.sharding import PartitionSpec as P

MESH = pl.DeviceIdType.MESH
F32 = jnp.float32
BF16 = jnp.bfloat16
TAPS = (1 / 16, 4 / 16, 6 / 16, 4 / 16, 1 / 16)


def down_rows(rows_in):
    m = np.zeros((rows_in // 2, rows_in), np.float32)
    for i in range(rows_in // 2):
        for t, tap in enumerate(TAPS):
            if 0 <= 2 * i + t - 2 < rows_in:
                m[i, 2 * i + t - 2] = tap
    return m


def up_rows(rows_in, rows_out, first):
    m = np.zeros((rows_out, rows_in), np.float32)
    for i in range(rows_out):
        k = first + i // 2
        pairs = ((k - 1, 1 / 8), (k, 6 / 8), (k + 1, 1 / 8)) if i % 2 == 0 else ((k, 1 / 2), (k + 1, 1 / 2))
        for r, tap in pairs:
            if 0 <= r < rows_in:
                m[i, r] = tap
    return m


def down_block():
    m = np.zeros((768, 256), np.float32)
    for o in range(256):
        for t, tap in enumerate(TAPS):
            m[128 + 2 * o + t - 2, o] = tap
    return m


def up_block():
    m = np.zeros((512, 512), np.float32)
    for k in range(256):
        m[127 + k, 2 * k] = m[129 + k, 2 * k] = 1 / 8
        m[128 + k, 2 * k] = 6 / 8
        m[128 + k, 2 * k + 1] = m[129 + k, 2 * k + 1] = 1 / 2
    return m


def twice(count, matrix):
    diagonal = np.kron(np.eye(count, dtype=np.float32), matrix)
    return np.concatenate([diagonal, diagonal], axis=1)


def dot(a, b):
    return lax.dot_general(a, b, (((1,), (0,)), ((), ())), preferred_element_type=F32)


def terms(v):
    high = v.astype(BF16)
    return high, (v - high.astype(F32)).astype(BF16)


def folded(v, stacked):
    if not stacked:
        return v
    rows = v.shape[0] // 2
    return v[:rows] + v[rows:]


def col_down(source, matrix, width, put, stacked=True):
    for j in range(width // 512):
        first = 512 * j - 128
        low, high = max(0, first), min(width, first + 768)
        taps = matrix[low - first : high - first, :]
        put(256 * j, 256, folded(dot(source(low, high), taps), stacked))


def col_up(source, matrix, width, put):
    for j in range(width // 256):
        first = 256 * j - 128
        low, high = max(0, first), min(width, first + 512)
        taps = matrix[low - first : high - first, :]
        put(512 * j, 512, folded(dot(source(low, high), taps), True))


def row_apply(matrix, read, width, put):
    for low in range(0, width, 512):
        put(low, 512, dot(matrix, jnp.concatenate(terms(read(low, low + 512)), axis=0)))


def kernel(
    n_rows, n_gz, planes, colours, strip, width,
    x_hbm, gain_ref, *refs,
):
    constants, out_ref, rest = refs[:9], refs[9], refs[10:]
    copied, rest = rest[:9], rest[9:]
    body(n_rows, n_gz, planes, colours, strip, width, x_hbm, gain_ref, constants, copied, out_ref, *rest)


def body(
    n_rows, n_gz, planes, colours, strip, width, x_hbm, gain_ref, constants, copied, out_ref,
    x_ref, x_sem, const_sem,
    grey, sq, xb, cext, l1, l2, st, up2, detail, logit, lse, lse_in, lse_fin, w0, cw, cw2, w1, w2, c1, part, part_in,
    h_send, h_recv, e_send, e_recv, eo_send, eo_recv, j_send, j_recv, jo_send, jo_recv,
    final, final_sem, *halos,
):
    image_halos, weight_halos = halos[:4], halos[4:]
    pc = planes * colours
    half, quarter = strip // 2, strip // 4
    ext0, ext1, ext2 = strip + 32, half + 16, quarter + 8
    w_half, w_quarter = width // 2, width // 4
    r = lax.axis_index("rows")
    z = lax.axis_index("gz")
    has_up, has_down = r > 0, r < n_rows - 1
    upper, lower = jnp.maximum(r - 1, 0), jnp.minimum(r + 1, n_rows - 1)
    left = z < n_gz // 2
    inward = jnp.where(left, z + 1, z - 1)
    has_outer = jnp.logical_and(z > 0, z < n_gz - 1)
    outward = jnp.where(has_outer, jnp.where(left, z - 1, z + 1), z)
    is_mid = jnp.logical_or(z == n_gz // 2 - 1, z == n_gz // 2)
    slot = jnp.where(is_mid, 1, 0)
    not_mid = jnp.logical_not(is_mid)

    dcol_ref, ucol_ref, d1x_ref, d1w_ref, d2x_ref, d2w_ref, u2x_ref, u2b_ref, u1_ref = copied
    loads = [pltpu.make_async_copy(x_hbm.at[p], x_ref.at[p], x_sem.at[p]) for p in range(planes)]
    fetches = [pltpu.make_async_copy(a, b, const_sem.at[k]) for k, (a, b) in enumerate(zip(constants, copied))]
    for copy in loads + fetches:
        copy.start()

    barrier = pltpu.get_barrier_semaphore()

    def greet(cond, device):
        @pl.when(cond)
        def _():
            pl.semaphore_signal(barrier, inc=1, device_id=device, device_id_type=MESH)

    greet(has_up, {"rows": upper})
    greet(has_down, {"rows": lower})
    greet(has_outer, {"gz": outward})
    pl.semaphore_signal(barrier, inc=1, device_id={"gz": inward}, device_id_type=MESH)

    for p in range(planes):
        loads[p].wait()
        samples = [x_ref[p, c].astype(F32) for c in range(colours)]
        for c in range(colours):
            xb[pl.ds((p * colours + c) * strip, strip), :] = samples[c].astype(BF16)
        mixed = 0.299 * samples[0] + 0.587 * samples[1] + 0.114 * samples[2]
        grey[p, pl.ds(8, strip), :width] = mixed * (1.0 / 255.0)
        grey[p, pl.ds(8, strip), width:] = jnp.zeros((strip, 128), F32)

    @pl.when(jnp.logical_not(has_up))
    def _():
        grey[:, 0:8, :] = jnp.zeros((planes, 8, width + 128), F32)

    @pl.when(jnp.logical_not(has_down))
    def _():
        grey[:, strip + 8 :, :] = jnp.zeros((planes, 8, width + 128), F32)

    for low in (0, strip + 16):
        cext[:, :, pl.ds(low, 16), :] = jnp.zeros((planes, colours, 16, w_half), F32)
        cw[:, pl.ds(low, 16), :] = jnp.zeros((planes, 16, w_half), F32)

    pl.semaphore_wait(
        barrier, 1 + has_up.astype(jnp.int32) + has_down.astype(jnp.int32) + has_outer.astype(jnp.int32)
    )

    def halo(kind, ref, lead, depth):
        def view(first):
            return ref.at[(slice(None),) * lead + (pl.ds(first, depth), slice(None))]

        def copies():
            up = pltpu.make_async_remote_copy(
                src_ref=view(depth), dst_ref=view(strip + depth),
                send_sem=h_send.at[kind, 0], recv_sem=h_recv.at[kind, 0],
                device_id={"rows": upper}, device_id_type=MESH,
            )
            down = pltpu.make_async_remote_copy(
                src_ref=view(strip), dst_ref=view(0),
                send_sem=h_send.at[kind, 1], recv_sem=h_recv.at[kind, 1],
                device_id={"rows": lower}, device_id_type=MESH,
            )
            return up, down

        def start():
            up, down = copies()
            pl.when(has_up)(up.start)
            pl.when(has_down)(down.start)

        def arrived():
            up, down = copies()
            pl.when(has_down)(up.wait_recv)
            pl.when(has_up)(down.wait_recv)

        def sent():
            up, down = copies()
            pl.when(has_up)(up.wait_send)
            pl.when(has_down)(down.wait_send)

        return start, arrived, sent

    def packed_halo(kind, arrays, to_up, to_down, from_up, from_down):
        def copies():
            up = pltpu.make_async_remote_copy(
                src_ref=to_up, dst_ref=from_down, send_sem=h_send.at[kind, 0], recv_sem=h_recv.at[kind, 0],
                device_id={"rows": upper}, device_id_type=MESH,
            )
            down = pltpu.make_async_remote_copy(
                src_ref=to_down, dst_ref=from_up, send_sem=h_send.at[kind, 1], recv_sem=h_recv.at[kind, 1],
                device_id={"rows": lower}, device_id_type=MESH,
            )
            return up, down

        def start():
            up, down = copies()

            @pl.when(has_up)
            def _():
                for i, (ref, lead) in enumerate(arrays):
                    to_up[pl.ds(11 * i, 11), :] = ref[lead + (pl.ds(16, 11), slice(None))]
                up.start()

            @pl.when(has_down)
            def _():
                for i, (ref, lead) in enumerate(arrays):
                    to_down[pl.ds(10 * i, 10), :] = ref[lead + (pl.ds(strip + 6, 10), slice(None))]
                down.start()

        def arrived():
            up, down = copies()

            @pl.when(has_down)
            def _():
                up.wait_recv()
                for i, (ref, lead) in enumerate(arrays):
                    ref[lead + (pl.ds(strip + 16, 11), slice(None))] = from_down[pl.ds(11 * i, 11), :]

            @pl.when(has_up)
            def _():
                down.wait_recv()
                for i, (ref, lead) in enumerate(arrays):
                    ref[lead + (pl.ds(6, 10), slice(None))] = from_up[pl.ds(10 * i, 10), :]

        def sent():
            up, down = copies()
            pl.when(has_up)(up.wait_send)
            pl.when(has_down)(down.wait_send)

        return start, arrived, sent

    def chain(own, arrive, final, send, recv, out_send, out_recv):
        def inner(view, k, s):
            return pltpu.make_async_remote_copy(
                src_ref=own.at[view], dst_ref=arrive.at[(s,) + view],
                send_sem=send.at[k], recv_sem=recv.at[s, k],
                device_id={"gz": inward}, device_id_type=MESH,
            )

        def outer(view, k):
            return pltpu.make_async_remote_copy(
                src_ref=final.at[view], dst_ref=final.at[view],
                send_sem=out_send.at[k], recv_sem=out_recv.at[k],
                device_id={"gz": outward}, device_id_type=MESH,
            )

        return inner, outer

    grey_start, grey_arrived, grey_sent = halo(0, grey, 1, 8)
    image_start, image_arrived, image_sent = packed_halo(
        1, [(cext, (p, c)) for p in range(planes) for c in range(colours)], *image_halos
    )
    weight_start, weight_arrived, weight_sent = packed_halo(2, [(cw, (p,)) for p in range(planes)], *weight_halos)
    e_inner, e_outer = chain(lse, lse_in, lse_fin, e_send, e_recv, eo_send, eo_recv)
    j_inner, j_outer = chain(part, part_in, final, j_send, j_recv, jo_send, jo_recv)

    grey_start()
    for copy in fetches:
        copy.wait()

    def put_c(low, count, v):
        cext[:, :, pl.ds(16, strip), low : low + count] = (v * (1.0 / 255.0)).reshape(planes, colours, strip, count)

    col_down(lambda a, b: xb[:, a:b], dcol_ref, width, put_c, False)
    image_start()

    padded = width + 128
    e_chunks = [(pl.ds(8 * t, 8), slice(None)) for t in range(strip // 8)]

    def square(p, i):
        line = lax.broadcasted_iota(jnp.int32, (8, padded), 0) + (r * strip - 4 + 8 * i)
        column = lax.broadcasted_iota(jnp.int32, (8, padded), 1)
        inside = (line >= 0) & (line < strip * n_rows) & (column < width)
        centre = grey[p, pl.ds(4 + 8 * i, 8), :]
        lap = 4.0 * centre - grey[p, pl.ds(3 + 8 * i, 8), :] - grey[p, pl.ds(5 + 8 * i, 8), :]
        lap = lap - pltpu.roll(centre, 1, 1) - pltpu.roll(centre, padded - 1, 1)
        lap = jnp.where(inside, lap, 0.0)
        sq[p, pl.ds(8 * i, 8), :] = lap * lap

    def merge(a, b):
        return jnp.maximum(a, b) + jnp.log(1.0 + jnp.exp(-jnp.abs(a - b)))

    def clarity(t):
        rows = pl.ds(8 * t, 8)
        top = None
        for p in range(planes):
            total = sq[p, rows, :]
            for k in range(1, 9):
                total = total + sq[p, pl.ds(8 * t + k, 8), :]
            two = total + pltpu.roll(total, 1, 1)
            four = two + pltpu.roll(two, 2, 1)
            eight = four + pltpu.roll(four, 4, 1)
            nine = eight + pltpu.roll(total, 8, 1)
            energy = pltpu.roll(nine, padded - 4, 1)
            scaled = energy[:, :width] * gain_ref[p]
            logit[p, rows, :] = scaled
            top = scaled if top is None else merge(top, scaled)
        lse[rows, :] = top

        @pl.when(jnp.logical_not(has_outer))
        def _():
            e_inner(e_chunks[t], t, slot).start()

    last = strip // 8
    for i in range(1, last):
        for p in range(planes):
            square(p, i)
    for t in range(1, last - 1):
        clarity(t)

    grey_arrived()
    for p in range(planes):
        square(p, 0)
        square(p, last)
    e_order = list(range(1, last - 1)) + sorted({0, last - 1})
    for t in e_order[last - 2 :]:
        clarity(t)

    @pl.when(has_outer)
    def _():
        for k in e_order:
            view = e_chunks[k]
            e_inner(view, k, 0).wait_recv()
            lse[view] = merge(lse[view], lse_in[(0,) + view])
            e_inner(view, k, slot).start()

    @pl.when(is_mid)
    def _():
        for k in e_order:
            view = e_chunks[k]
            e_inner(view, k, 1).wait_recv()
            lse_fin[view] = merge(lse[view], lse_in[(1,) + view])
            pl.when(has_outer)(e_outer(view, k).start)

    image_arrived()

    def edge_mask(rows_ext, margin, rows_own):
        row = lax.broadcasted_iota(jnp.int32, (rows_ext, 512), 0) + (r * rows_own - margin)
        return ((row >= 0) & (row < rows_own * n_rows)).astype(F32)[None]

    mask1 = edge_mask(ext1, 8, half)
    mask2 = edge_mask(ext2, 4, quarter)
    for p in range(planes):
        def put_l1(low, count, v):
            l1[p, :, :, low : low + count] = v.reshape(colours, ext1, count) * mask1

        row_apply(d1x_ref[...], lambda a, b: cext[p, :, :, a:b].reshape(colours * ext0, b - a), w_half, put_l1)

    def stage(rows, low, count, v, base=0):
        size = v.shape[0]
        high, rest = terms(v)
        st[pl.ds(base, size), low : low + count] = high
        st[pl.ds(rows + base, size), low : low + count] = rest

    def staged(rows):
        return lambda a, b: st[0 : 2 * rows, a:b]

    full = colours * strip
    for p in range(planes):
        row_apply(
            u1_ref[...], lambda a, b: l1[p, :, :, a:b].reshape(colours * ext1, b - a), w_half,
            functools.partial(stage, planes * full, base=p * full),
        )

    def put_detail(low, count, v):
        samples = xb[:, low : low + count].astype(F32)
        detail[:, :, :, low : low + count] = (samples * (1.0 / 255.0) - v).reshape(planes, colours, strip, count)

    col_up(staged(planes * full), ucol_ref, w_half, put_detail)

    @pl.when(not_mid)
    def _():
        for k in e_order:
            e_outer(e_chunks[k], k).wait_recv()
            pl.when(has_outer)(e_outer(e_chunks[k], k).start)

    for t in range(strip // 8):
        view = e_chunks[t]
        for p in range(planes):
            w0[(p,) + view] = jnp.exp(logit[(p,) + view] - lse_fin[view])

    own_rows = planes * strip
    for low in range(0, width, 512):
        stage(own_rows, low, 512, w0[:, :, low : low + 512].reshape(own_rows, 512))

    def put_cw(low, count, v):
        cw[:, pl.ds(16, strip), low : low + count] = v.reshape(planes, strip, count)

    col_down(staged(own_rows), dcol_ref, width, put_cw)
    weight_start()

    for low in range(0, width, 512):
        for c in range(colours):
            acc = w0[0, :, low : low + 512] * detail[0, c, :, low : low + 512]
            for p in range(1, planes):
                acc = acc + w0[p, :, low : low + 512] * detail[p, c, :, low : low + 512]
            part[c, :, low : low + 512] = acc

    rows1 = pc * ext1
    for low in range(0, w_half, 512):
        stage(rows1, low, 512, l1[:, :, :, low : low + 512].reshape(rows1, 512))

    def put_c2(low, count, v):
        up2[:, low : low + count] = v

    col_down(staged(rows1), dcol_ref, w_half, put_c2)

    def put_l2(low, count, v):
        l2[:, :, :, low : low + count] = (v.reshape(pc, ext2, count) * mask2).reshape(planes, colours, ext2, count)

    row_apply(d2x_ref[...], lambda a, b: up2[:, a:b], w_quarter, put_l2)
    row_apply(
        u2x_ref[...], lambda a, b: l2[:, :, :, a:b].reshape(pc * ext2, b - a), w_quarter,
        functools.partial(stage, rows1),
    )

    def put_up2(low, count, v):
        up2[:, low : low + count] = v

    col_up(staged(rows1), ucol_ref, w_quarter, put_up2)

    weight_arrived()
    w_rows = planes * ext0

    def put_w1(low, count, v):
        w1[:, :, low : low + count] = v.reshape(planes, ext1, count) * mask1

    row_apply(d1w_ref[...], lambda a, b: cw[:, :, a:b].reshape(w_rows, b - a), w_half, put_w1)
    w1_rows = planes * ext1
    for low in range(0, w_half, 512):
        stage(w1_rows, low, 512, w1[:, :, low : low + 512].reshape(w1_rows, 512))

    def put_cw2(low, count, v):
        cw2[:, low : low + count] = v

    col_down(staged(w1_rows), dcol_ref, w_half, put_cw2)

    def put_w2(low, count, v):
        w2[:, :, low : low + count] = v.reshape(planes, ext2, count) * mask2

    row_apply(d2w_ref[...], lambda a, b: cw2[:, a:b], w_quarter, put_w2)

    def read_b2(a, b):
        acc = w2[0, :, a:b][None] * l2[0, :, :, a:b]
        for p in range(1, planes):
            acc = acc + w2[p, :, a:b][None] * l2[p, :, :, a:b]
        return acc.reshape(colours * ext2, b - a)

    rows_c1 = colours * ext1
    row_apply(u2b_ref[...], read_b2, w_quarter, functools.partial(stage, rows_c1))

    def put_c1(low, count, v):
        acc = v.reshape(colours, ext1, count)
        for p in range(planes):
            first = p * rows_c1
            coarse = up2[pl.ds(first, rows_c1), low : low + count].reshape(colours, ext1, count)
            acc = acc + w1[p, :, low : low + count][None] * (l1[p, :, :, low : low + count] - coarse)
        c1[:, :, low : low + count] = acc * mask1

    col_up(staged(rows_c1), ucol_ref, w_quarter, put_c1)

    row_apply(
        u1_ref[...], lambda a, b: c1[:, :, a:b].reshape(rows_c1, b - a), w_half, functools.partial(stage, full)
    )

    j_chunks = [(c, slice(None), slice(low, low + 512)) for low in range(0, width, 512) for c in range(colours)]

    def into(k):
        view = j_chunks[k]

        @pl.when(has_outer)
        def _():
            j_inner(view, k, 0).wait_recv()
            part[view] = part[view] + part_in[(0,) + view]
            j_inner(view, k, slot).start()

    lag = 3

    def store(k):
        return pltpu.make_async_copy(final.at[j_chunks[k]], out_ref.at[j_chunks[k]], final_sem.at[k])

    def step(k):
        if k < len(j_chunks):
            into(k)
        if k >= lag:
            view = j_chunks[k - lag]

            @pl.when(is_mid)
            def _():
                j_inner(view, k - lag, 1).wait_recv()
                final[view] = part[view] + part_in[(1,) + view]
                pl.when(has_outer)(j_outer(view, k - lag).start)
                store(k - lag).start()

    def put_part(low, count, v):
        part[:, :, low : low + count] += v.reshape(colours, strip, count)

        @pl.when(jnp.logical_not(has_outer))
        def _():
            for c in range(colours):
                k = low // count * colours + c
                j_inner(j_chunks[k], k, slot).start()

        for k in range(max(0, low // count - 1) * colours, low // count * colours):
            step(k)

    col_up(staged(full), ucol_ref, w_half, put_part)

    for k in range(len(j_chunks) - colours, len(j_chunks) + lag):
        step(k)

    @pl.when(not_mid)
    def _():
        for k, view in enumerate(j_chunks):
            j_outer(view, k).wait_recv()
            pl.when(has_outer)(j_outer(view, k).start)
            store(k).start()

    grey_sent()
    image_sent()
    weight_sent()
    for k, view in enumerate(e_chunks):
        e_inner(view, k, slot).wait_send()
        pl.when(has_outer)(e_outer(view, k).wait_send)
    for k, view in enumerate(j_chunks):
        j_inner(view, k, slot).wait_send()
        store(k).wait()
        pl.when(has_outer)(j_outer(view, k).wait_send)


def on_device(n_rows, n_gz, samples, gain):
    planes, colours, strip, width = samples.shape
    pc = planes * colours
    half, quarter = strip // 2, strip // 4
    ext0, ext1, ext2 = strip + 32, half + 16, quarter + 8
    d1, d2 = down_rows(ext0), down_rows(ext1)
    u2, u1 = up_rows(ext2, ext1, 0), up_rows(ext1, strip, 8)
    constants = [
        down_block(), up_block(), twice(colours, d1), twice(planes, d1), twice(pc, d2), twice(planes, d2),
        twice(pc, u2), twice(colours, u2), twice(colours, u1),
    ]
    constants = [jnp.asarray(c.astype(ml_dtypes.bfloat16)) for c in constants]
    n_e, n_j = strip // 8, colours * width // 512
    dma = pltpu.SemaphoreType.DMA
    hbm = pl.BlockSpec(memory_space=pltpu.HBM)
    return pl.pallas_call(
        functools.partial(kernel, n_rows, n_gz, planes, colours, strip, width),
        out_shape=jax.ShapeDtypeStruct((colours, strip, width), F32),
        in_specs=[hbm, pl.BlockSpec(memory_space=pltpu.SMEM)] + [hbm] * len(constants),
        out_specs=hbm,
        scratch_shapes=[pltpu.VMEM(c.shape, c.dtype) for c in constants] + [
            pltpu.VMEM(samples.shape, samples.dtype),
            dma((planes,)), dma((len(constants),)),
            pltpu.VMEM((planes, strip + 16, width + 128), F32),
            pltpu.VMEM((planes, strip + 8, width + 128), F32),
            pltpu.VMEM((pc * strip, width), BF16),
            pltpu.VMEM((planes, colours, ext0, width // 2), F32),
            pltpu.VMEM((planes, colours, ext1, width // 2), F32),
            pltpu.VMEM((planes, colours, ext2, width // 4), F32),
            pltpu.VMEM((2 * max(pc * ext1, pc * strip), width), BF16),
            pltpu.VMEM((pc * ext1, width // 2), F32),
            pltpu.VMEM((planes, colours, strip, width), F32),
            pltpu.VMEM((planes, strip, width), F32),
            pltpu.VMEM((strip, width), F32),
            pltpu.VMEM((2, strip, width), F32),
            pltpu.VMEM((strip, width), F32),
            pltpu.VMEM((planes, strip, width), F32),
            pltpu.VMEM((planes, ext0, width // 2), F32),
            pltpu.VMEM((planes * ext1, width // 4), F32),
            pltpu.VMEM((planes, ext1, width // 2), F32),
            pltpu.VMEM((planes, ext2, width // 4), F32),
            pltpu.VMEM((colours, ext1, width // 2), F32),
            pltpu.VMEM((colours, strip, width), F32),
            pltpu.VMEM((2, colours, strip, width), F32),
            dma((3, 2)), dma((3, 2)),
            dma((n_e,)), dma((2, n_e)), dma((n_e,)), dma((n_e,)),
            dma((n_j,)), dma((2, n_j)), dma((n_j,)), dma((n_j,)),
            pltpu.VMEM((colours, strip, width), F32), dma((n_j,)),
        ] + [
            pltpu.VMEM((-(-count * rows // 8) * 8, width // 2), F32)
            for count in (pc, planes) for rows in (11, 10, 10, 11)
        ],
        compiler_params=pltpu.CompilerParams(
            collective_id=0, has_side_effects=True, vmem_limit_bytes=56 * 1024 * 1024
        ),
    )(samples, gain, *constants)


def solution(mesh):
    return jax.shard_map(
        functools.partial(on_device, mesh.shape["rows"], mesh.shape["gz"]),
        mesh=mesh,
        in_specs=(P("gz", None, "rows", None), P("gz")),
        out_specs=P(None, "rows", None),
        check_vma=False,
    )
```

```python
import functools

import jax
import jax.numpy as jnp
import ml_dtypes
import numpy as np
from jax import lax
from jax.experimental import pallas as pl
from jax.experimental.pallas import tpu as pltpu
from jax.sharding import PartitionSpec as P

MESH = pl.DeviceIdType.MESH
F32 = jnp.float32
BF16 = jnp.bfloat16
TAPS = (1 / 16, 4 / 16, 6 / 16, 4 / 16, 1 / 16)


def down_rows(rows_in):
    m = np.zeros((rows_in // 2, rows_in), np.float32)
    for i in range(rows_in // 2):
        for t, tap in enumerate(TAPS):
            if 0 <= 2 * i + t - 2 < rows_in:
                m[i, 2 * i + t - 2] = tap
    return m


def up_rows(rows_in, rows_out, first):
    m = np.zeros((rows_out, rows_in), np.float32)
    for i in range(rows_out):
        k = first + i // 2
        pairs = ((k - 1, 1 / 8), (k, 6 / 8), (k + 1, 1 / 8)) if i % 2 == 0 else ((k, 1 / 2), (k + 1, 1 / 2))
        for r, tap in pairs:
            if 0 <= r < rows_in:
                m[i, r] = tap
    return m


def down_block():
    m = np.zeros((768, 256), np.float32)
    for o in range(256):
        for t, tap in enumerate(TAPS):
            m[128 + 2 * o + t - 2, o] = tap
    return m


def up_block():
    m = np.zeros((512, 512), np.float32)
    for k in range(256):
        m[127 + k, 2 * k] = m[129 + k, 2 * k] = 1 / 8
        m[128 + k, 2 * k] = 6 / 8
        m[128 + k, 2 * k + 1] = m[129 + k, 2 * k + 1] = 1 / 2
    return m


def twice(count, matrix):
    diagonal = np.kron(np.eye(count, dtype=np.float32), matrix)
    return np.concatenate([diagonal, diagonal], axis=1)


def dot(a, b):
    return lax.dot_general(a, b, (((1,), (0,)), ((), ())), preferred_element_type=F32)


def terms(v):
    high = v.astype(BF16)
    return high, (v - high.astype(F32)).astype(BF16)


def folded(v, stacked):
    if not stacked:
        return v
    rows = v.shape[0] // 2
    return v[:rows] + v[rows:]


def col_down(source, matrix, width, put, stacked=True):
    for j in range(width // 512):
        first = 512 * j - 128
        low, high = max(0, first), min(width, first + 768)
        taps = matrix[low - first : high - first, :]
        put(256 * j, 256, folded(dot(source(low, high), taps), stacked))


def col_up(source, matrix, width, put):
    for j in range(width // 256):
        first = 256 * j - 128
        low, high = max(0, first), min(width, first + 512)
        taps = matrix[low - first : high - first, :]
        put(512 * j, 512, folded(dot(source(low, high), taps), True))


def row_apply(matrix, read, width, put):
    for low in range(0, width, 512):
        put(low, 512, dot(matrix, jnp.concatenate(terms(read(low, low + 512)), axis=0)))


def kernel(
    n_rows, n_gz, planes, colours, strip, width,
    x_hbm, gain_ref, *refs,
):
    constants, out_ref, rest = refs[:9], refs[9], refs[10:]
    copied, rest = rest[:9], rest[9:]
    body(n_rows, n_gz, planes, colours, strip, width, x_hbm, gain_ref, constants, copied, out_ref, *rest)


def body(
    n_rows, n_gz, planes, colours, strip, width, x_hbm, gain_ref, constants, copied, out_ref,
    x_ref, x_sem, const_sem,
    grey, sq, xb, cext, l1, l2, st, up2, detail, logit, lse, lse_in, lse_fin, w0, cw, cw2, w1, w2, c1, part, part_in,
    h_send, h_recv, e_send, e_recv, eo_send, eo_recv, j_send, j_recv, jo_send, jo_recv,
    final, final_sem, *halos,
):
    image_halos, weight_halos = halos[:4], halos[4:]
    pc = planes * colours
    half, quarter = strip // 2, strip // 4
    ext0, ext1, ext2 = strip + 32, half + 16, quarter + 8
    w_half, w_quarter = width // 2, width // 4
    r = lax.axis_index("rows")
    z = lax.axis_index("gz")
    has_up, has_down = r > 0, r < n_rows - 1
    upper, lower = jnp.maximum(r - 1, 0), jnp.minimum(r + 1, n_rows - 1)
    left = z < n_gz // 2
    inward = jnp.where(left, z + 1, z - 1)
    has_outer = jnp.logical_and(z > 0, z < n_gz - 1)
    outward = jnp.where(has_outer, jnp.where(left, z - 1, z + 1), z)
    is_mid = jnp.logical_or(z == n_gz // 2 - 1, z == n_gz // 2)
    slot = jnp.where(is_mid, 1, 0)
    not_mid = jnp.logical_not(is_mid)

    dcol_ref, ucol_ref, d1x_ref, d1w_ref, d2x_ref, d2w_ref, u2x_ref, u2b_ref, u1_ref = copied
    loads = [pltpu.make_async_copy(x_hbm.at[p], x_ref.at[p], x_sem.at[p]) for p in range(planes)]
    fetches = [pltpu.make_async_copy(a, b, const_sem.at[k]) for k, (a, b) in enumerate(zip(constants, copied))]
    for copy in loads + fetches:
        copy.start()

    barrier = pltpu.get_barrier_semaphore()

    def greet(cond, device):
        @pl.when(cond)
        def _():
            pl.semaphore_signal(barrier, inc=1, device_id=device, device_id_type=MESH)

    greet(has_up, {"rows": upper})
    greet(has_down, {"rows": lower})
    greet(has_outer, {"gz": outward})
    pl.semaphore_signal(barrier, inc=1, device_id={"gz": inward}, device_id_type=MESH)

    for p in range(planes):
        loads[p].wait()
        samples = [x_ref[p, c].astype(F32) for c in range(colours)]
        for c in range(colours):
            xb[pl.ds((p * colours + c) * strip, strip), :] = samples[c].astype(BF16)
        mixed = 0.299 * samples[0] + 0.587 * samples[1] + 0.114 * samples[2]
        grey[p, pl.ds(8, strip), :width] = mixed * (1.0 / 255.0)
        grey[p, pl.ds(8, strip), width:] = jnp.zeros((strip, 128), F32)

    @pl.when(jnp.logical_not(has_up))
    def _():
        grey[:, 0:8, :] = jnp.zeros((planes, 8, width + 128), F32)

    @pl.when(jnp.logical_not(has_down))
    def _():
        grey[:, strip + 8 :, :] = jnp.zeros((planes, 8, width + 128), F32)

    for low in (0, strip + 16):
        cext[:, :, pl.ds(low, 16), :] = jnp.zeros((planes, colours, 16, w_half), F32)
        cw[:, pl.ds(low, 16), :] = jnp.zeros((planes, 16, w_half), F32)

    pl.semaphore_wait(
        barrier, 1 + has_up.astype(jnp.int32) + has_down.astype(jnp.int32) + has_outer.astype(jnp.int32)
    )

    def halo(kind, ref, lead, depth):
        def view(first):
            return ref.at[(slice(None),) * lead + (pl.ds(first, depth), slice(None))]

        def copies():
            up = pltpu.make_async_remote_copy(
                src_ref=view(depth), dst_ref=view(strip + depth),
                send_sem=h_send.at[kind, 0], recv_sem=h_recv.at[kind, 0],
                device_id={"rows": upper}, device_id_type=MESH,
            )
            down = pltpu.make_async_remote_copy(
                src_ref=view(strip), dst_ref=view(0),
                send_sem=h_send.at[kind, 1], recv_sem=h_recv.at[kind, 1],
                device_id={"rows": lower}, device_id_type=MESH,
            )
            return up, down

        def start():
            up, down = copies()
            pl.when(has_up)(up.start)
            pl.when(has_down)(down.start)

        def arrived():
            up, down = copies()
            pl.when(has_down)(up.wait_recv)
            pl.when(has_up)(down.wait_recv)

        def sent():
            up, down = copies()
            pl.when(has_up)(up.wait_send)
            pl.when(has_down)(down.wait_send)

        return start, arrived, sent

    def packed_halo(kind, arrays, to_up, to_down, from_up, from_down):
        def copies():
            up = pltpu.make_async_remote_copy(
                src_ref=to_up, dst_ref=from_down, send_sem=h_send.at[kind, 0], recv_sem=h_recv.at[kind, 0],
                device_id={"rows": upper}, device_id_type=MESH,
            )
            down = pltpu.make_async_remote_copy(
                src_ref=to_down, dst_ref=from_up, send_sem=h_send.at[kind, 1], recv_sem=h_recv.at[kind, 1],
                device_id={"rows": lower}, device_id_type=MESH,
            )
            return up, down

        def start():
            up, down = copies()

            @pl.when(has_up)
            def _():
                for i, (ref, lead) in enumerate(arrays):
                    to_up[pl.ds(11 * i, 11), :] = ref[lead + (pl.ds(16, 11), slice(None))]
                up.start()

            @pl.when(has_down)
            def _():
                for i, (ref, lead) in enumerate(arrays):
                    to_down[pl.ds(10 * i, 10), :] = ref[lead + (pl.ds(strip + 6, 10), slice(None))]
                down.start()

        def arrived():
            up, down = copies()

            @pl.when(has_down)
            def _():
                up.wait_recv()
                for i, (ref, lead) in enumerate(arrays):
                    ref[lead + (pl.ds(strip + 16, 11), slice(None))] = from_down[pl.ds(11 * i, 11), :]

            @pl.when(has_up)
            def _():
                down.wait_recv()
                for i, (ref, lead) in enumerate(arrays):
                    ref[lead + (pl.ds(6, 10), slice(None))] = from_up[pl.ds(10 * i, 10), :]

        def sent():
            up, down = copies()
            pl.when(has_up)(up.wait_send)
            pl.when(has_down)(down.wait_send)

        return start, arrived, sent

    def chain(own, arrive, final, send, recv, out_send, out_recv):
        def inner(view, k, s):
            return pltpu.make_async_remote_copy(
                src_ref=own.at[view], dst_ref=arrive.at[(s,) + view],
                send_sem=send.at[k], recv_sem=recv.at[s, k],
                device_id={"gz": inward}, device_id_type=MESH,
            )

        def outer(view, k):
            return pltpu.make_async_remote_copy(
                src_ref=final.at[view], dst_ref=final.at[view],
                send_sem=out_send.at[k], recv_sem=out_recv.at[k],
                device_id={"gz": outward}, device_id_type=MESH,
            )

        return inner, outer

    grey_start, grey_arrived, grey_sent = halo(0, grey, 1, 8)
    image_start, image_arrived, image_sent = packed_halo(
        1, [(cext, (p, c)) for p in range(planes) for c in range(colours)], *image_halos
    )
    weight_start, weight_arrived, weight_sent = packed_halo(2, [(cw, (p,)) for p in range(planes)], *weight_halos)
    e_inner, e_outer = chain(lse, lse_in, lse_fin, e_send, e_recv, eo_send, eo_recv)
    j_inner, j_outer = chain(part, part_in, final, j_send, j_recv, jo_send, jo_recv)

    grey_start()
    padded = width + 128
    e_chunks = [(pl.ds(8 * t, 8), slice(None)) for t in range(strip // 8)]

    def square(p, i):
        line = lax.broadcasted_iota(jnp.int32, (8, padded), 0) + (r * strip - 4 + 8 * i)
        column = lax.broadcasted_iota(jnp.int32, (8, padded), 1)
        inside = (line >= 0) & (line < strip * n_rows) & (column < width)
        centre = grey[p, pl.ds(4 + 8 * i, 8), :]
        lap = 4.0 * centre - grey[p, pl.ds(3 + 8 * i, 8), :] - grey[p, pl.ds(5 + 8 * i, 8), :]
        lap = lap - pltpu.roll(centre, 1, 1) - pltpu.roll(centre, padded - 1, 1)
        lap = jnp.where(inside, lap, 0.0)
        sq[p, pl.ds(8 * i, 8), :] = lap * lap

    def merge(a, b):
        return jnp.maximum(a, b) + jnp.log(1.0 + jnp.exp(-jnp.abs(a - b)))

    def clarity(t):
        rows = pl.ds(8 * t, 8)
        top = None
        for p in range(planes):
            total = sq[p, rows, :]
            for k in range(1, 9):
                total = total + sq[p, pl.ds(8 * t + k, 8), :]
            two = total + pltpu.roll(total, 1, 1)
            four = two + pltpu.roll(two, 2, 1)
            eight = four + pltpu.roll(four, 4, 1)
            nine = eight + pltpu.roll(total, 8, 1)
            energy = pltpu.roll(nine, padded - 4, 1)
            scaled = energy[:, :width] * gain_ref[p]
            logit[p, rows, :] = scaled
            top = scaled if top is None else merge(top, scaled)
        lse[rows, :] = top

        @pl.when(jnp.logical_not(has_outer))
        def _():
            e_inner(e_chunks[t], t, slot).start()

    last = strip // 8
    for i in range(1, last):
        for p in range(planes):
            square(p, i)
    for t in range(1, last - 1):
        clarity(t)

    for copy in fetches:
        copy.wait()

    def put_c(low, count, v):
        cext[:, :, pl.ds(16, strip), low : low + count] = (v * (1.0 / 255.0)).reshape(planes, colours, strip, count)

    col_down(lambda a, b: xb[:, a:b], dcol_ref, width, put_c, False)
    image_start()

    e_order = list(range(1, last - 1)) + sorted({0, last - 1})

    def forward(chunks):
        @pl.when(has_outer)
        def _():
            for k in chunks:
                view = e_chunks[k]
                e_inner(view, k, 0).wait_recv()
                lse[view] = merge(lse[view], lse_in[(0,) + view])
                e_inner(view, k, slot).start()

    forward(e_order[: last - 2])
    grey_arrived()
    for p in range(planes):
        square(p, 0)
        square(p, last)
    for t in e_order[last - 2 :]:
        clarity(t)

    forward(e_order[last - 2 :])

    @pl.when(is_mid)
    def _():
        for k in e_order:
            view = e_chunks[k]
            e_inner(view, k, 1).wait_recv()
            lse_fin[view] = merge(lse[view], lse_in[(1,) + view])
            pl.when(has_outer)(e_outer(view, k).start)

    image_arrived()

    def edge_mask(rows_ext, margin, rows_own):
        row = lax.broadcasted_iota(jnp.int32, (rows_ext, 512), 0) + (r * rows_own - margin)
        return ((row >= 0) & (row < rows_own * n_rows)).astype(F32)[None]

    mask1 = edge_mask(ext1, 8, half)
    mask2 = edge_mask(ext2, 4, quarter)
    for p in range(planes):
        def put_l1(low, count, v):
            l1[p, :, :, low : low + count] = v.reshape(colours, ext1, count) * mask1

        row_apply(d1x_ref[...], lambda a, b: cext[p, :, :, a:b].reshape(colours * ext0, b - a), w_half, put_l1)

    def stage(rows, low, count, v, base=0):
        size = v.shape[0]
        high, rest = terms(v)
        st[pl.ds(base, size), low : low + count] = high
        st[pl.ds(rows + base, size), low : low + count] = rest

    def staged(rows):
        return lambda a, b: st[0 : 2 * rows, a:b]

    full = colours * strip
    for p in range(planes):
        row_apply(
            u1_ref[...], lambda a, b: l1[p, :, :, a:b].reshape(colours * ext1, b - a), w_half,
            functools.partial(stage, planes * full, base=p * full),
        )

    def put_detail(low, count, v):
        samples = xb[:, low : low + count].astype(F32)
        detail[:, :, :, low : low + count] = (samples * (1.0 / 255.0) - v).reshape(planes, colours, strip, count)

    col_up(staged(planes * full), ucol_ref, w_half, put_detail)

    @pl.when(not_mid)
    def _():
        for k in e_order:
            e_outer(e_chunks[k], k).wait_recv()
            pl.when(has_outer)(e_outer(e_chunks[k], k).start)

    for t in range(strip // 8):
        view = e_chunks[t]
        for p in range(planes):
            w0[(p,) + view] = jnp.exp(logit[(p,) + view] - lse_fin[view])

    own_rows = planes * strip
    for low in range(0, width, 512):
        stage(own_rows, low, 512, w0[:, :, low : low + 512].reshape(own_rows, 512))

    def put_cw(low, count, v):
        cw[:, pl.ds(16, strip), low : low + count] = v.reshape(planes, strip, count)

    col_down(staged(own_rows), dcol_ref, width, put_cw)
    weight_start()

    for low in range(0, width, 512):
        for c in range(colours):
            acc = w0[0, :, low : low + 512] * detail[0, c, :, low : low + 512]
            for p in range(1, planes):
                acc = acc + w0[p, :, low : low + 512] * detail[p, c, :, low : low + 512]
            part[c, :, low : low + 512] = acc

    rows1 = pc * ext1
    for low in range(0, w_half, 512):
        stage(rows1, low, 512, l1[:, :, :, low : low + 512].reshape(rows1, 512))

    def put_c2(low, count, v):
        up2[:, low : low + count] = v

    col_down(staged(rows1), dcol_ref, w_half, put_c2)

    def put_l2(low, count, v):
        l2[:, :, :, low : low + count] = (v.reshape(pc, ext2, count) * mask2).reshape(planes, colours, ext2, count)

    row_apply(d2x_ref[...], lambda a, b: up2[:, a:b], w_quarter, put_l2)
    row_apply(
        u2x_ref[...], lambda a, b: l2[:, :, :, a:b].reshape(pc * ext2, b - a), w_quarter,
        functools.partial(stage, rows1),
    )

    def put_up2(low, count, v):
        up2[:, low : low + count] = v

    col_up(staged(rows1), ucol_ref, w_quarter, put_up2)

    weight_arrived()
    w_rows = planes * ext0

    def put_w1(low, count, v):
        w1[:, :, low : low + count] = v.reshape(planes, ext1, count) * mask1

    row_apply(d1w_ref[...], lambda a, b: cw[:, :, a:b].reshape(w_rows, b - a), w_half, put_w1)
    w1_rows = planes * ext1
    for low in range(0, w_half, 512):
        stage(w1_rows, low, 512, w1[:, :, low : low + 512].reshape(w1_rows, 512))

    def put_cw2(low, count, v):
        cw2[:, low : low + count] = v

    col_down(staged(w1_rows), dcol_ref, w_half, put_cw2)

    def put_w2(low, count, v):
        w2[:, :, low : low + count] = v.reshape(planes, ext2, count) * mask2

    row_apply(d2w_ref[...], lambda a, b: cw2[:, a:b], w_quarter, put_w2)

    def read_b2(a, b):
        acc = w2[0, :, a:b][None] * l2[0, :, :, a:b]
        for p in range(1, planes):
            acc = acc + w2[p, :, a:b][None] * l2[p, :, :, a:b]
        return acc.reshape(colours * ext2, b - a)

    rows_c1 = colours * ext1
    row_apply(u2b_ref[...], read_b2, w_quarter, functools.partial(stage, rows_c1))

    def put_c1(low, count, v):
        acc = v.reshape(colours, ext1, count)
        for p in range(planes):
            first = p * rows_c1
            coarse = up2[pl.ds(first, rows_c1), low : low + count].reshape(colours, ext1, count)
            acc = acc + w1[p, :, low : low + count][None] * (l1[p, :, :, low : low + count] - coarse)
        c1[:, :, low : low + count] = acc * mask1

    col_up(staged(rows_c1), ucol_ref, w_quarter, put_c1)

    row_apply(
        u1_ref[...], lambda a, b: c1[:, :, a:b].reshape(rows_c1, b - a), w_half, functools.partial(stage, full)
    )

    j_chunks = [(c, slice(None), slice(low, low + 512)) for low in range(0, width, 512) for c in range(colours)]

    def into(k):
        view = j_chunks[k]

        @pl.when(has_outer)
        def _():
            j_inner(view, k, 0).wait_recv()
            part[view] = part[view] + part_in[(0,) + view]
            j_inner(view, k, slot).start()

    lag = 3

    def store(k):
        return pltpu.make_async_copy(final.at[j_chunks[k]], out_ref.at[j_chunks[k]], final_sem.at[k])

    def step(k):
        if k < len(j_chunks):
            into(k)
        if k >= lag:
            view = j_chunks[k - lag]

            @pl.when(is_mid)
            def _():
                j_inner(view, k - lag, 1).wait_recv()
                final[view] = part[view] + part_in[(1,) + view]
                pl.when(has_outer)(j_outer(view, k - lag).start)
                store(k - lag).start()

    def put_part(low, count, v):
        part[:, :, low : low + count] += v.reshape(colours, strip, count)

        @pl.when(jnp.logical_not(has_outer))
        def _():
            for c in range(colours):
                k = low // count * colours + c
                j_inner(j_chunks[k], k, slot).start()

        for k in range(max(0, low // count - 1) * colours, low // count * colours):
            step(k)

    col_up(staged(full), ucol_ref, w_half, put_part)

    for k in range(len(j_chunks) - colours, len(j_chunks) + lag):
        step(k)

    @pl.when(not_mid)
    def _():
        for k, view in enumerate(j_chunks):
            j_outer(view, k).wait_recv()
            pl.when(has_outer)(j_outer(view, k).start)
            store(k).start()

    grey_sent()
    image_sent()
    weight_sent()
    for k, view in enumerate(e_chunks):
        e_inner(view, k, slot).wait_send()
        pl.when(has_outer)(e_outer(view, k).wait_send)
    for k, view in enumerate(j_chunks):
        j_inner(view, k, slot).wait_send()
        store(k).wait()
        pl.when(has_outer)(j_outer(view, k).wait_send)


def on_device(n_rows, n_gz, samples, gain):
    planes, colours, strip, width = samples.shape
    pc = planes * colours
    half, quarter = strip // 2, strip // 4
    ext0, ext1, ext2 = strip + 32, half + 16, quarter + 8
    d1, d2 = down_rows(ext0), down_rows(ext1)
    u2, u1 = up_rows(ext2, ext1, 0), up_rows(ext1, strip, 8)
    constants = [
        down_block(), up_block(), twice(colours, d1), twice(planes, d1), twice(pc, d2), twice(planes, d2),
        twice(pc, u2), twice(colours, u2), twice(colours, u1),
    ]
    constants = [jnp.asarray(c.astype(ml_dtypes.bfloat16)) for c in constants]
    n_e, n_j = strip // 8, colours * width // 512
    dma = pltpu.SemaphoreType.DMA
    hbm = pl.BlockSpec(memory_space=pltpu.HBM)
    return pl.pallas_call(
        functools.partial(kernel, n_rows, n_gz, planes, colours, strip, width),
        out_shape=jax.ShapeDtypeStruct((colours, strip, width), F32),
        in_specs=[hbm, pl.BlockSpec(memory_space=pltpu.SMEM)] + [hbm] * len(constants),
        out_specs=hbm,
        scratch_shapes=[pltpu.VMEM(c.shape, c.dtype) for c in constants] + [
            pltpu.VMEM(samples.shape, samples.dtype),
            dma((planes,)), dma((len(constants),)),
            pltpu.VMEM((planes, strip + 16, width + 128), F32),
            pltpu.VMEM((planes, strip + 8, width + 128), F32),
            pltpu.VMEM((pc * strip, width), BF16),
            pltpu.VMEM((planes, colours, ext0, width // 2), F32),
            pltpu.VMEM((planes, colours, ext1, width // 2), F32),
            pltpu.VMEM((planes, colours, ext2, width // 4), F32),
            pltpu.VMEM((2 * max(pc * ext1, pc * strip), width), BF16),
            pltpu.VMEM((pc * ext1, width // 2), F32),
            pltpu.VMEM((planes, colours, strip, width), F32),
            pltpu.VMEM((planes, strip, width), F32),
            pltpu.VMEM((strip, width), F32),
            pltpu.VMEM((2, strip, width), F32),
            pltpu.VMEM((strip, width), F32),
            pltpu.VMEM((planes, strip, width), F32),
            pltpu.VMEM((planes, ext0, width // 2), F32),
            pltpu.VMEM((planes * ext1, width // 4), F32),
            pltpu.VMEM((planes, ext1, width // 2), F32),
            pltpu.VMEM((planes, ext2, width // 4), F32),
            pltpu.VMEM((colours, ext1, width // 2), F32),
            pltpu.VMEM((colours, strip, width), F32),
            pltpu.VMEM((2, colours, strip, width), F32),
            dma((3, 2)), dma((3, 2)),
            dma((n_e,)), dma((2, n_e)), dma((n_e,)), dma((n_e,)),
            dma((n_j,)), dma((2, n_j)), dma((n_j,)), dma((n_j,)),
            pltpu.VMEM((colours, strip, width), F32), dma((n_j,)),
        ] + [
            pltpu.VMEM((-(-count * rows // 8) * 8, width // 2), F32)
            for count in (pc, planes) for rows in (11, 10, 10, 11)
        ],
        compiler_params=pltpu.CompilerParams(
            collective_id=0, has_side_effects=True, vmem_limit_bytes=56 * 1024 * 1024
        ),
    )(samples, gain, *constants)


def solution(mesh):
    return jax.shard_map(
        functools.partial(on_device, mesh.shape["rows"], mesh.shape["gz"]),
        mesh=mesh,
        in_specs=(P("gz", None, "rows", None), P("gz")),
        out_specs=P(None, "rows", None),
        check_vma=False,
    )
```
